128 devices in a mesh: rep: 2 (over z_hi), shard: 64 (over y, z_lo, x, core).
Axes of the slice: x: 4, y: 4, z: 4 (z_hi: 2, z_lo: 2; z = z_hi * 2 + z_lo), core: 2. Of those that a mesh axis runs over, the one named last changes fastest.
Arguments:
- tokens: bfloat16 [16384, 2048], P(('rep', 'shard')), may hold values from -6 to 6
- cotangent: bfloat16 [16384, 2048], P(('rep', 'shard')), may hold values from -6 to 6
- segment_ids: int32 [16384], P(('rep', 'shard')), may hold values from 1 to 16384, as said below
- position_ids: int32 [16384], P(('rep', 'shard')), may hold values from 0 to 1023, as said below
- w_qkv: float32 [2048, 2560], P('shard'), may hold values from -0.125 to 0.125
- w_out: float32 [2048, 2048], P('shard'), may hold values from -1.5 to 1.5
- w_gate_up: float32 [2048, 11264], P('shard'), may hold values from -0.125 to 0.125
- w_down: float32 [5632, 2048], P('shard'), may hold values from -0.078125 to 0.078125
- gains: float32 [2, 2048], P(None, 'shard'), may hold values from 0.5 to 1.5
- m_qkv: float32 [2048, 2560], P('shard'), may hold values from -80 to 80
- v_qkv: float32 [2048, 2560], P('shard'), may hold values from 425.984 to 6881.28
- m_out: float32 [2048, 2048], P('shard'), may hold values from -8 to 8
- v_out: float32 [2048, 2048], P('shard'), may hold values from 4.308992 to 68.8128
- m_gate_up: float32 [2048, 11264], P('shard'), may hold values from -24 to 24
- v_gate_up: float32 [2048, 11264], P('shard'), may hold values from 38.83008 to 620.9536
- m_down: float32 [5632, 2048], P('shard'), may hold values from -40 to 40
- v_down: float32 [5632, 2048], P('shard'), may hold values from 107.80672 to 1720.32
- m_gains: float32 [2, 2048], P(None, 'shard'), may hold values from -80 to 80
- v_gains: float32 [2, 2048], P(None, 'shard'), may hold values from 425.984 to 6881.28
Outputs:
- mixed: float32 [16384, 2048], P(('rep', 'shard'))
- d_tokens: float32 [16384, 2048], P(('rep', 'shard'))
- new_qkv: float32 [2048, 2560], P('shard')
- new_m_qkv: float32 [2048, 2560], P('shard')
- new_v_qkv: float32 [2048, 2560], P('shard')
- new_out: float32 [2048, 2048], P('shard')
- new_m_out: float32 [2048, 2048], P('shard')
- new_v_out: float32 [2048, 2048], P('shard')
- new_gate_up: float32 [2048, 11264], P('shard')
- new_m_gate_up: float32 [2048, 11264], P('shard')
- new_v_gate_up: float32 [2048, 11264], P('shard')
- new_down: float32 [5632, 2048], P('shard')
- new_m_down: float32 [5632, 2048], P('shard')
- new_v_down: float32 [5632, 2048], P('shard')
- new_gains: float32 [2, 2048], P(None, 'shard')
- new_m_gains: float32 [2, 2048], P(None, 'shard')
- new_v_gains: float32 [2, 2048], P(None, 'shard')
The draws below stay inside these ranges and needn't reach their ends.
Inputs may be any that keep to these rules, and one draw needn't show every extreme that they name: `segment_ids`: tokens form sequences of 1024 consecutive tokens; documents never cross a sequence's end; every document but a sequence's last holds 200 tokens or more; numbers rise along the tokens, and no two documents share one; the last document of the k-th sequence (from 0) is numbered (k + 1) * 1024; in each draw one sequence is a single document. `position_ids`: positions count from 0 at each document's first token.
All inputs are finite; a program needn't handle non-finite values.
Results may differ from the reference program's by a relative error of at most 0.02.
Values may be sent and summed in bfloat16 or wider, within the bound.
No kernel may reach another device: no remote copies, remote signals or barrier semaphores. Data moves between devices by JAX's collectives and lax.ppermute only.
A program may use at most 448 MiB of HBM per device.

```python
import math
import jax
import jax.numpy as jnp
from jax import lax

D = 2048
HEADS = 32
KV_HEADS = 4
HEAD_DIM = 64
FF = 5632
DOC_MIN = 200
STEP = 10
ATT = 2048
QKV = 2560
LEN = 1024
TOKENS = 16384
SEQS = 16


def doc_layout(key):
    seq_count = TOKENS // LEN
    pieces = LEN // DOC_MIN + 1
    lengths = jax.random.randint(jax.random.fold_in(key, 11), (seq_count, pieces), DOC_MIN, LEN + 1)
    ends = jnp.cumsum(lengths, axis=1)
    single = jax.random.randint(jax.random.fold_in(key, 12), (), 0, seq_count)
    ends = jnp.where(jnp.arange(seq_count)[:, None] == single, jnp.full_like(ends, LEN), ends)
    places = jnp.arange(LEN)
    local_doc = jnp.sum((ends[:, None, :] <= places[None, :, None]).astype(jnp.int32), axis=2)
    before = jnp.take_along_axis(ends, jnp.maximum(local_doc - 1, 0), axis=1)
    starts = jnp.where(local_doc > 0, before, 0)
    positions = places[None, :] - starts
    last_doc = local_doc[:, LEN - 1:LEN]
    numbers = (jnp.arange(seq_count)[:, None] + 1) * LEN - (last_doc - local_doc)
    return (numbers.reshape(-1).astype(jnp.int32), positions.reshape(-1).astype(jnp.int32))


def draw_segment_ids(key, part):
    layout = doc_layout(key)
    return layout[0]


def draw_position_ids(key, part):
    layout = doc_layout(key)
    return layout[1]


def steps_of(key, shape, cuts, least, largest):
    level, own = 1.0, jax.random.fold_in(key, 6)
    for position, blocks in cuts:
        heights = jnp.exp(jax.random.uniform(jax.random.fold_in(own, position), (blocks,), jnp.float32, least / len(cuts), largest / len(cuts)))
        level = level * jnp.repeat(heights, shape[position] // blocks).reshape([-1 if axis == position else 1 for axis in range(len(shape))])
    return level


def normal_values(key, dims, spread, limit, shards=(), held_as=jnp.bfloat16):
    factor_of = steps_of(key, dims, shards, -0.22, 0.18) if shards else 1.0
    result = jax.random.normal(key, dims, jnp.float32) * spread * factor_of
    return jnp.minimum(jnp.maximum(result, -limit), limit).astype(held_as)


def setup_inputs(seed: int = 0) -> dict:
    seeds = jax.random.split(jax.random.key(seed), 20)
    return {
        "tokens": normal_values(seeds[0], (TOKENS, D), 1.0, 6.0, ((0, 128),)),
        "cotangent": normal_values(seeds[1], (TOKENS, D), 1.0, 6.0, ((0, 128),)),
        "segment_ids": draw_segment_ids(jax.random.fold_in(seeds[19], 71), 0),
        "position_ids": draw_position_ids(jax.random.fold_in(seeds[19], 71), 0),
        "w_qkv": normal_values(seeds[4], (D, QKV), D ** -0.5, 0.125, ((0, 64),), jnp.float32),
        "w_out": normal_values(seeds[5], (ATT, D), (ATT * 8 // LEN) ** -0.5, 1.5, ((0, 64),), jnp.float32),
        "w_gate_up": normal_values(seeds[6], (D, 2 * FF), D ** -0.5, 0.125, ((0, 64),), jnp.float32),
        "w_down": normal_values(seeds[7], (FF, D), FF ** -0.5, 0.078125, ((0, 64),), jnp.float32),
        "gains": jnp.clip(1.0 + 0.1 * jax.random.normal(seeds[8], (2, D), jnp.float32), 0.5, 1.5),
        "m_qkv": normal_values(seeds[9], (D, QKV), (0.111 * TOKENS ** 0.5), 80.0, ((0, 64),), jnp.float32),
        "v_qkv": jnp.clip(jnp.exp(math.log(6881.28) - 2.7821581 * jax.random.uniform(seeds[10], (D, QKV), jnp.float32) ** steps_of(seeds[10], (D, QKV), ((0, 64),), -0.2, 0.2)), 425.984, 6881.28),
        "m_out": normal_values(seeds[11], (ATT, D), (0.0111 * TOKENS ** 0.5), 8.0, ((0, 64),), jnp.float32),
        "v_out": jnp.clip(jnp.exp(math.log(68.8128) - 2.77068576 * jax.random.uniform(seeds[12], (ATT, D), jnp.float32) ** steps_of(seeds[12], (ATT, D), ((0, 64),), -0.2, 0.2)), 4.308992, 68.8128),
        "m_gate_up": normal_values(seeds[13], (D, 2 * FF), (0.0333 * TOKENS ** 0.5), 24.0, ((0, 64),), jnp.float32),
        "v_gate_up": jnp.clip(jnp.exp(math.log(620.9536) - 2.772061 * jax.random.uniform(seeds[14], (D, 2 * FF), jnp.float32) ** steps_of(seeds[14], (D, 2 * FF), ((0, 64),), -0.2, 0.2)), 38.83008, 620.9536),
        "m_down": normal_values(seeds[15], (FF, D), (0.0555 * TOKENS ** 0.5), 40.0, ((0, 64),), jnp.float32),
        "v_down": jnp.clip(jnp.exp(math.log(1720.32) - 2.7699256 * jax.random.uniform(seeds[16], (FF, D), jnp.float32) ** steps_of(seeds[16], (FF, D), ((0, 64),), -0.2, 0.2)), 107.80672, 1720.32),
        "m_gains": normal_values(seeds[17], (2, D), (0.111 * TOKENS ** 0.5), 80.0, ((1, 64),), jnp.float32),
        "v_gains": jnp.clip(jnp.exp(math.log(6881.28) - 2.7821581 * jax.random.uniform(seeds[18], (2, D), jnp.float32) ** steps_of(seeds[18], (2, D), ((1, 64),), -0.2, 0.2)), 425.984, 6881.28),
    }


EPSILON = 1e-05
BETA_ONE = 0.9
BETA_TWO = 0.95
ADAM_EPSILON = 1e-08
DECAY = 0.1
RATE_QKV = 0.02
RATE_OUT = 0.25
RATE_GATE_UP = 0.02
RATE_DOWN = 0.013
RATE_GAINS = 0.3
HIGHEST = lax.Precision.HIGHEST

@jax.custom_vjp
def low(v):
    return lax.optimization_barrier(v.astype(jnp.bfloat16)).astype(jnp.float32)

@jax.custom_vjp
def low_back(v):
    return v

def low_keep(v):
    return (low(v), None)

def low_pass(kept, grad):
    return (grad,)

def back_keep(v):
    return (v, None)

def back_low(kept, grad):
    return (low(grad),)
low.defvjp(low_keep, low_pass)
low_back.defvjp(back_keep, back_low)

def rms_norm(values, gain):
    return values * lax.rsqrt(lax.optimization_barrier(jnp.mean(values * values, axis=-1, keepdims=True)) + EPSILON) * gain

def rotate_pairs(values, positions):
    half = values.shape[-1] // 2
    freqs = 10000.0 ** (-jnp.arange(half).astype(jnp.float32) * 2.0 / values.shape[-1])
    angles = positions.astype(jnp.float32)[:, None] * freqs[None, :]
    cosine = jnp.cos(angles)[:, None, :]
    sine = jnp.sin(angles)[:, None, :]
    first = values[..., :half]
    second = values[..., half:]
    return jnp.concatenate([first * cosine - second * sine, second * cosine + first * sine], axis=-1)

def attend(block):
    queries, keys, values, segments, positions = block
    scores = jnp.einsum('qgrd,kgd->grqk', queries, keys, precision=HIGHEST) * HEAD_DIM ** (-0.5)
    scores = low_back(scores)
    allowed = (segments[:, None] == segments[None, :]) & (positions[None, :] <= positions[:, None])
    scores = jnp.where(allowed[None, None], scores, -1e+30)
    probs = low(jax.nn.softmax(scores, axis=-1))
    return jnp.einsum('grqk,kgd->qgrd', probs, values, precision=HIGHEST)

def block_forward(inputs, w_qkv, w_out, w_gate_up, w_down, gains, segment_ids, position_ids):
    gain_low = low(gains)
    kv_width = KV_HEADS * HEAD_DIM
    ratio = HEADS // KV_HEADS
    normed = low(rms_norm(inputs, gain_low[0]))
    projected = low_back(jnp.dot(normed, low(w_qkv), precision=HIGHEST))
    queries = rotate_pairs(projected[:, :ATT].reshape(TOKENS, HEADS, HEAD_DIM), position_ids)
    queries = low(queries).reshape(SEQS, LEN, KV_HEADS, ratio, HEAD_DIM)
    keys = rotate_pairs(projected[:, ATT:ATT + kv_width].reshape(TOKENS, KV_HEADS, HEAD_DIM), position_ids)
    keys = low(keys).reshape(SEQS, LEN, KV_HEADS, HEAD_DIM)
    values = low(projected[:, ATT + kv_width:]).reshape(SEQS, LEN, KV_HEADS, HEAD_DIM)
    attended = lax.map(jax.checkpoint(attend), (queries, keys, values, segment_ids.reshape(SEQS, LEN), position_ids.reshape(SEQS, LEN)))
    heads_out = low(low_back(attended.reshape(TOKENS, ATT)))
    middle = inputs + low_back(jnp.dot(heads_out, low(w_out), precision=HIGHEST))
    normed_two = low(rms_norm(middle, gain_low[1]))
    gate_up = low_back(jnp.dot(normed_two, low(w_gate_up), precision=HIGHEST))
    hidden = low(jax.nn.silu(gate_up[:, :FF]) * gate_up[:, FF:])
    return middle + low_back(jnp.dot(hidden, low(w_down), precision=HIGHEST))

def adam_step(weight, grad, first, second, rate):
    first_new = BETA_ONE * first + (1.0 - BETA_ONE) * grad
    second_new = BETA_TWO * second + (1.0 - BETA_TWO) * grad * grad
    first_hat = first_new / (1.0 - BETA_ONE ** STEP)
    second_hat = second_new / (1.0 - BETA_TWO ** STEP)
    weight_new = weight - rate * (first_hat / (jnp.sqrt(second_hat) + ADAM_EPSILON) + DECAY * weight)
    return (weight_new, first_new, second_new)

def reference(tokens, cotangent, segment_ids, position_ids, w_qkv, w_out, w_gate_up, w_down, gains, m_qkv, v_qkv, m_out, v_out, m_gate_up, v_gate_up, m_down, v_down, m_gains, v_gains):

    def forward(inputs, wa, wb, wc, wd, gn):
        return block_forward(inputs, wa, wb, wc, wd, gn, segment_ids, position_ids)
    mixed, backward = jax.vjp(forward, tokens.astype(jnp.float32), w_qkv, w_out, w_gate_up, w_down, gains)
    grads = backward(cotangent.astype(jnp.float32))
    qkv_new = adam_step(w_qkv, grads[1], m_qkv, v_qkv, RATE_QKV)
    out_new = adam_step(w_out, grads[2], m_out, v_out, RATE_OUT)
    gate_new = adam_step(w_gate_up, grads[3], m_gate_up, v_gate_up, RATE_GATE_UP)
    down_new = adam_step(w_down, grads[4], m_down, v_down, RATE_DOWN)
    gains_new = adam_step(gains, grads[5], m_gains, v_gains, RATE_GAINS)
    return (mixed, grads[0], qkv_new[0], qkv_new[1], qkv_new[2], out_new[0], out_new[1], out_new[2], gate_new[0], gate_new[1], gate_new[2], down_new[0], down_new[1], down_new[2], gains_new[0], gains_new[1], gains_new[2])
```

```python
import jax
import jax.numpy as jnp
from jax import lax
from jax.experimental import pallas as pl
from jax.experimental.pallas import tpu as pltpu
from jax.sharding import PartitionSpec as P

HEADS = 32
KV_HEADS = 4
HEAD_DIM = 64
D = 2048
FF = 5632
STEP = 10
ROWS = 128
GROUP = 8
TOK = ROWS * GROUP
HALF = TOK // 2
HEADS_HERE = HEADS // GROUP
Q_HERE = HEADS_HERE * HEAD_DIM
PROJ_HERE = Q_HERE + 2 * HEAD_DIM
FF_HERE = FF // GROUP
Q_BLOCK = 256

EPSILON = 1e-05
BETA_ONE = 0.9
BETA_TWO = 0.95
ADAM_EPSILON = 1e-08
DECAY = 0.1
RATE_QKV = 0.02
RATE_OUT = 0.25
RATE_GATE_UP = 0.02
RATE_DOWN = 0.013
RATE_GAINS = 0.3

BF = jnp.bfloat16
F32 = jnp.float32
BOTH = ("rep", "shard")
LINES = [[8 * b + a for a in range(8)] for b in range(8)]
COLUMNS = [[16 * y + r for y in range(4)] for r in range(16)]


def index_of(r, y, z, x, c):
    return r * 64 + y * 16 + z * 8 + x * 2 + c


def places():
    return [
        (r, y, z, x, c)
        for r in range(2)
        for y in range(4)
        for z in range(2)
        for x in range(4)
        for c in range(2)
    ]


def come_from(v, y=0, x=0, c=0, zz=0):
    pairs = []
    for r, yy, z, xx, cc in places():
        ring = (2 * r + z + zz) % 4
        source = index_of(ring // 2, (yy + y) % 4, ring % 2, (xx + x) % 4, cc ^ c)
        pairs.append((source, index_of(r, yy, z, xx, cc)))
    return lax.ppermute(v, BOTH, pairs)


def turned(v):
    pairs = [(index_of(r, x, c, y, z), index_of(r, y, z, x, c)) for r, y, z, x, c in places()]
    return lax.ppermute(v, BOTH, pairs)


def dot(left, right):
    return jnp.dot(left, right, preferred_element_type=F32)


def dot_nt(left, right):
    return lax.dot_general(left, right, (((1,), (1,)), ((), ())), preferred_element_type=F32)


def dot_tn(left, right):
    return lax.dot_general(left, right, (((0,), (0,)), ((), ())), preferred_element_type=F32)


def line_gather(v):
    near = jnp.concatenate([v] + [come_from(v, x=k) for k in (1, 2, 3)], axis=0)
    return near, come_from(near, c=1)


def line_scatter(near, far, product):
    came = come_from(product(far).astype(BF), c=1)
    mine = product(near) + came.astype(F32)
    low = mine[ROWS:].astype(BF)
    total = mine[:ROWS]
    for k in (1, 2, 3):
        total = total + come_from(low[(k - 1) * ROWS : k * ROWS], x=-k).astype(F32)
    return total


def column_exchange(v):
    return lax.all_to_all(v, "shard", 0, 0, tiled=True, axis_index_groups=COLUMNS)


def plane_gather(v, axis):
    z = (lax.axis_index("shard") // 8) % 2
    column = column_exchange(jnp.broadcast_to(v[None], (4, *v.shape)))
    first, second = jnp.split(column, 2, axis=axis + 1)
    other = jnp.concatenate([come_from(first, zz=1), come_from(second, zz=3)], axis=axis + 1)
    full = jnp.where(
        z == 0, jnp.stack([column, other], axis=1), jnp.stack([other, column], axis=1)
    )
    return full.reshape(8 * v.shape[0], v.shape[1])


def plane_scatter(v, axis):
    z = (lax.axis_index("shard") // 8) % 2
    blocks = v.reshape(4, 2, v.shape[0] // 8, v.shape[1])
    mine = lax.dynamic_index_in_dim(blocks, z, 1, keepdims=False)
    theirs = lax.dynamic_index_in_dim(blocks, 1 - z, 1, keepdims=False)
    first, second = jnp.split(theirs, 2, axis=axis + 1)
    came = jnp.concatenate([come_from(first, zz=1), come_from(second, zz=3)], axis=axis + 1)
    total = (mine.astype(F32) + came.astype(F32)).astype(BF)
    result = jnp.sum(column_exchange(total).astype(F32), axis=0)
    return result + come_from(result.astype(BF), zz=2).astype(F32)


def line_exchange(v):
    return lax.all_to_all(v, "shard", 0, 0, tiled=True, axis_index_groups=LINES)


def rate_of(values):
    return lax.rsqrt(jnp.mean(values * values, axis=-1, keepdims=True) + EPSILON)


def unit_norm(values):
    return values * rate_of(values)


def unit_norm_back(values, grad):
    rate = rate_of(values)
    unit = values * rate
    return rate * (grad - unit * jnp.mean(grad * unit, axis=-1, keepdims=True))


def gated_unit(gate, upward):
    return jax.nn.silu(gate) * upward


def adam_step(weight, grad, first, second, rate):
    first_new = BETA_ONE * first + (1.0 - BETA_ONE) * grad
    second_new = BETA_TWO * second + (1.0 - BETA_TWO) * grad * grad
    first_hat = first_new / (1.0 - BETA_ONE**STEP)
    second_hat = second_new / (1.0 - BETA_TWO**STEP)
    weight_new = weight - rate * (
        first_hat / (jnp.sqrt(second_hat) + ADAM_EPSILON) + DECAY * weight
    )
    return (weight_new, first_new, second_new)


def lanes(rows):
    return lax.broadcasted_iota(jnp.int32, (rows, 128), 1)


def rotated(v, cosine, sine, lane):
    partner = jnp.where(lane % HEAD_DIM < HEAD_DIM // 2, pltpu.roll(v, 96, 1), pltpu.roll(v, 32, 1))
    return v * cosine + partner * sine


def split_pair(pair, k_ref, v_ref, lane):
    swapped = pltpu.roll(pair, 64, 1)
    low = lane < HEAD_DIM
    zero = jnp.zeros_like(pair)
    k_ref[0] = jnp.where(low, pair, zero).astype(BF)
    k_ref[1] = jnp.where(low, zero, swapped).astype(BF)
    v_ref[0] = jnp.where(low, swapped, zero).astype(BF)
    v_ref[1] = jnp.where(low, zero, pair).astype(BF)


def barred(column_ref, row_ref):
    same = column_ref[:, 0:1] == row_ref[0:1, :]
    before = row_ref[1:2, :] <= column_ref[:, 1:2]
    return jnp.where(same & before, 0.0, -1e30)


def forward_kernel(
    proj_ref, pair_ref, cos_ref, sin_ref, cos_all_ref, sin_all_ref, column_ref, row_ref,
    out_ref, q_ref, kv_ref, total_ref, k_scr, v_scr,
):
    lane = lanes(Q_BLOCK)

    @pl.when(pl.program_id(0) == 0)
    def _():
        wide = lanes(TOK)
        pair = pair_ref[...]
        turned_pair = rotated(pair, cos_all_ref[...], sin_all_ref[...], wide)
        pair = jnp.where(wide < HEAD_DIM, turned_pair, pair).astype(BF)
        kv_ref[...] = pair
        split_pair(pair.astype(F32), k_scr, v_scr, wide)

    bar = barred(column_ref, row_ref)
    totals = jnp.zeros((Q_BLOCK, 128), F32)
    for chunk in range(HEADS_HERE // 2):
        span = slice(128 * chunk, 128 * (chunk + 1))
        queries = rotated(proj_ref[:, span], cos_ref[...], sin_ref[...], lane).astype(BF)
        queries = (queries.astype(F32) * HEAD_DIM**-0.5).astype(BF)
        q_ref[:, span] = queries
        out = jnp.zeros((Q_BLOCK, 128), F32)
        for side in range(2):
            scores = dot_nt(queries, k_scr[side]) + bar
            peak = jnp.max(scores, axis=1, keepdims=True)
            expo = jnp.exp(scores - peak)
            total = jnp.sum(expo, axis=1, keepdims=True)
            probs = (expo * (1.0 / total)).astype(BF)
            out = out + dot(probs, v_scr[side])
            totals = jnp.where(lane == 2 * chunk + side, peak + jnp.log(total), totals)
        out_ref[:, span] = out.astype(BF)
    total_ref[...] = totals


def backward_kernel(
    do_ref, q_ref, kv_ref, total_ref, cos_ref, sin_ref, cos_all_ref, sin_all_ref, column_ref, row_ref,
    dq_ref, dkv_ref, k_scr, v_scr, dk_scr, dv_scr,
):
    lane = lanes(Q_BLOCK)
    step = pl.program_id(0)

    @pl.when(step == 0)
    def _():
        split_pair(kv_ref[...].astype(F32), k_scr, v_scr, lanes(TOK))
        dk_scr[...] = jnp.zeros_like(dk_scr)
        dv_scr[...] = jnp.zeros_like(dv_scr)

    bar = barred(column_ref, row_ref)
    for chunk in range(HEADS_HERE // 2):
        span = slice(128 * chunk, 128 * (chunk + 1))
        queries = q_ref[:, span]
        grads = do_ref[:, span]
        dq = jnp.zeros((Q_BLOCK, 128), F32)
        for side in range(2):
            held = (lane >= HEAD_DIM) == (side == 1)
            head = 2 * chunk + side
            scores = dot_nt(queries, k_scr[side]) + bar
            probs = jnp.exp(scores - total_ref[:, head : head + 1])
            dp = dot_nt(grads, v_scr[side])
            inner = jnp.sum(probs * dp, axis=1, keepdims=True)
            ds = (probs * (dp - inner)).astype(BF)
            dq = dq + dot(ds, k_scr[side])
            dk_scr[...] += dot_tn(ds, jnp.where(held, queries, jnp.zeros_like(queries)))
            dv_scr[...] += dot_tn(
                probs.astype(BF), jnp.where(held, grads, jnp.zeros_like(grads))
            )
        dq = dq * HEAD_DIM**-0.5
        dq_ref[:, span] = rotated(dq, cos_ref[...], -sin_ref[...], lane).astype(BF)

    @pl.when(step == pl.num_programs(0) - 1)
    def _():
        wide = lanes(TOK)
        dk = dk_scr[...] + pltpu.roll(dk_scr[...], 64, 1)
        dv = dv_scr[...] + pltpu.roll(dv_scr[...], 64, 1)
        dk = rotated(dk, cos_all_ref[...], -sin_all_ref[...], wide)
        dkv_ref[...] = jnp.where(wide < HEAD_DIM, dk, dv).astype(BF)


def blocked(cols):
    return pl.BlockSpec((Q_BLOCK, cols), lambda i: (i, 0))


def whole(rows, cols):
    return pl.BlockSpec((rows, cols), lambda i: (0, 0))


def attend(projected, cosine, sine, column, row):
    return pl.pallas_call(
        forward_kernel,
        grid=(TOK // Q_BLOCK,),
        in_specs=[
            blocked(Q_HERE),
            pl.BlockSpec((TOK, 128), lambda i: (0, Q_HERE // 128)),
            blocked(128),
            blocked(128),
            whole(TOK, 128),
            whole(TOK, 128),
            blocked(2),
            whole(2, TOK),
        ],
        out_specs=[blocked(Q_HERE), blocked(Q_HERE), whole(TOK, 128), blocked(128)],
        out_shape=[
            jax.ShapeDtypeStruct((TOK, Q_HERE), BF),
            jax.ShapeDtypeStruct((TOK, Q_HERE), BF),
            jax.ShapeDtypeStruct((TOK, 128), BF),
            jax.ShapeDtypeStruct((TOK, 128), F32),
        ],
        scratch_shapes=[pltpu.VMEM((2, TOK, 128), BF), pltpu.VMEM((2, TOK, 128), BF)],
        compiler_params=pltpu.CompilerParams(vmem_limit_bytes=40 * 2**20),
        cost_estimate=pl.CostEstimate(
            flops=8 * TOK * TOK * 128 * 2, bytes_accessed=6 * 2**20, transcendentals=4 * TOK * TOK
        ),
        name="attention_forward",
    )(projected, projected, cosine, sine, cosine, sine, column, row)


def attend_back(grads, queries, pair, totals, cosine, sine, column, row):
    return pl.pallas_call(
        backward_kernel,
        grid=(TOK // Q_BLOCK,),
        in_specs=[
            blocked(Q_HERE),
            blocked(Q_HERE),
            whole(TOK, 128),
            blocked(128),
            blocked(128),
            blocked(128),
            whole(TOK, 128),
            whole(TOK, 128),
            blocked(2),
            whole(2, TOK),
        ],
        out_specs=[blocked(Q_HERE), whole(TOK, 128)],
        out_shape=[
            jax.ShapeDtypeStruct((TOK, Q_HERE), BF),
            jax.ShapeDtypeStruct((TOK, 128), BF),
        ],
        scratch_shapes=[
            pltpu.VMEM((2, TOK, 128), BF),
            pltpu.VMEM((2, TOK, 128), BF),
            pltpu.VMEM((TOK, 128), F32),
            pltpu.VMEM((TOK, 128), F32),
        ],
        compiler_params=pltpu.CompilerParams(vmem_limit_bytes=40 * 2**20),
        cost_estimate=pl.CostEstimate(
            flops=20 * TOK * TOK * 128 * 2, bytes_accessed=6 * 2**20, transcendentals=4 * TOK * TOK
        ),
        name="attention_backward",
    )(grads, queries, pair, totals, cosine, sine, cosine, sine, column, row)


def small_rows(segment_ids, position_ids):
    parts = [position_ids // 32, position_ids % 32, segment_ids // 128, segment_ids % 128]
    flat = jnp.concatenate([p.astype(BF) for p in parts] + [jnp.zeros((256,), BF)])
    return jnp.concatenate([flat.reshape(2, PROJ_HERE), jnp.zeros((6, PROJ_HERE), BF)], axis=0)


def small_read(rows):
    s = lax.axis_index("shard")
    x, c = (s // 2) % 4, s % 2
    line = rows[:, :2].reshape(4, 2, 6, 128).astype(F32)
    line = lax.dynamic_slice(jnp.concatenate([line, line], axis=0), (x, 0, 0, 0), (4, 2, 6, 128))
    line = jnp.where(c == 0, line, line[:, ::-1]).transpose(1, 0, 2, 3).reshape(8, 6, 128)
    position = (line[:, 0] * 32.0 + line[:, 1]).reshape(TOK)
    segment = (line[:, 2] * 128.0 + line[:, 3]).reshape(TOK)
    return position, segment


def on_device(
    tokens,
    cotangent,
    segment_ids,
    position_ids,
    w_qkv,
    w_out,
    w_gate_up,
    w_down,
    gains,
    m_qkv,
    v_qkv,
    m_out,
    v_out,
    m_gate_up,
    v_gate_up,
    m_down,
    v_down,
    m_gains,
    v_gains,
):
    gain_rows = gains.astype(BF).astype(F32).T
    qkv_low = w_qkv.astype(BF).astype(F32)
    gate_low = w_gate_up.astype(BF).astype(F32)

    with jax.named_scope("qkv_weights_line"):
        low = (qkv_low * gain_rows[:, 0:1]).astype(BF)
        q_cols = low[:, :D].reshape(32, 8, Q_HERE)
        kv_cols = low[:, D:].reshape(32, 2, KV_HEADS, HEAD_DIM).transpose(0, 2, 1, 3)
        kv_cols = jnp.repeat(kv_cols.reshape(32, KV_HEADS, 2 * HEAD_DIM), 2, axis=1)
        qkv_cut = jnp.concatenate([q_cols, kv_cols], axis=2).transpose(1, 0, 2)
        small = jnp.broadcast_to(small_rows(segment_ids, position_ids)[None], (8, 8, PROJ_HERE))
        qkv_line = line_exchange(jnp.concatenate([qkv_cut, small], axis=1))
        positions, segments = small_read(qkv_line[:, 32:])
    with jax.named_scope("tokens_line"):
        tokens_halves = line_gather(tokens)
    with jax.named_scope("qkv_weights_plane"):
        qkv_full = plane_gather(qkv_line[:, :32].reshape(256, -1), 0)
    with jax.named_scope("out_down_turn"):
        out_down = turned(jnp.concatenate([w_out.astype(BF), w_down.astype(BF)], axis=0))
    with jax.named_scope("out_weights_plane"):
        out_full = plane_gather(out_down[:32], 1)
    with jax.named_scope("gate_weights_line"):
        low = (gate_low * gain_rows[:, 1:2]).astype(BF)
        gate_cut = low.reshape(32, 2, 8, FF_HERE).transpose(2, 0, 1, 3)
        gate_line = line_exchange(gate_cut.reshape(8, 32, -1)).reshape(256, -1)
    with jax.named_scope("gate_weights_plane"):
        gate_full = plane_gather(gate_line, 0)
    with jax.named_scope("down_weights_plane"):
        down_full = plane_gather(out_down[32:], 1)
    with jax.named_scope("cotangent_line"):
        cotangent_halves = line_gather(cotangent)

    freqs = 10000.0 ** (-jnp.arange(HEAD_DIM // 2).astype(F32) * 2.0 / HEAD_DIM)
    angles = positions[:, None] * freqs[None, :]
    cosine = jnp.tile(jnp.cos(angles), (1, 4))
    sine = jnp.sin(angles)
    sine = jnp.concatenate([-sine, sine, -sine, sine], axis=1)
    row = jnp.stack([segments, positions])
    column = row.T
    with jax.named_scope("projections"):
        normed = [unit_norm(t.astype(F32)).astype(BF) for t in tokens_halves]
        projected = jnp.concatenate([dot(n, qkv_full) for n in normed], axis=0)
    heads_out, queries, pair, totals = attend(projected, cosine, sine, column, row)
    inputs = tokens.astype(F32)
    with jax.named_scope("heads_out_line"):
        middle = inputs + line_scatter(
            heads_out[:HALF], heads_out[HALF:], lambda v: dot(v, out_full)
        )

    with jax.named_scope("normed_two_line"):
        normed_two = line_gather(unit_norm(middle).astype(BF))
    hidden, grad_gu = [], []
    for rows, grads in zip(normed_two, cotangent_halves):
        with jax.named_scope("feed_forward"):
            gate_up = dot(rows, gate_full)
            hid, back = jax.vjp(gated_unit, gate_up[:, :FF_HERE], gate_up[:, FF_HERE:])
            hidden.append(hid.astype(BF))
            grad_gu.append(jnp.concatenate(back(dot_nt(grads, down_full)), axis=1).astype(BF))
    with jax.named_scope("grad_normed_two_line"):
        grad_unit = line_scatter(*grad_gu, lambda v: dot_nt(v, gate_full))
        grad_middle = cotangent.astype(F32) + unit_norm_back(middle, grad_unit)
    with jax.named_scope("grad_attn_line"):
        grad_attn = line_gather(grad_middle.astype(BF))
    with jax.named_scope("mixed_line"):
        mixed = middle + line_scatter(*hidden, lambda v: dot(v, down_full))
    with jax.named_scope("grad_gate_plane"):
        grad_gate = dot_tn(jnp.concatenate(normed_two), jnp.concatenate(grad_gu)).astype(BF)
        grad_gate = plane_scatter(grad_gate, 0).astype(BF)
    with jax.named_scope("grad_gate_line"):
        grad_gate = line_exchange(grad_gate.reshape(8, 32, 2 * FF_HERE)).astype(F32)
        grad_gate = grad_gate.reshape(8, 32, 2, FF_HERE).transpose(1, 2, 0, 3).reshape(32, 2 * FF)
    with jax.named_scope("grad_down_plane"):
        grad_down = dot_tn(jnp.concatenate(hidden), jnp.concatenate(cotangent_halves)).astype(BF)
        grad_down = turned(plane_scatter(grad_down, 1).astype(BF)).astype(F32)

    with jax.named_scope("grad_heads"):
        grad_heads = jnp.concatenate([dot_nt(g, out_full) for g in grad_attn], axis=0).astype(BF)
    grad_q, grad_kv = attend_back(
        grad_heads, queries, pair, totals, cosine, sine, column, row
    )
    grad_proj = jnp.concatenate([grad_q, grad_kv], axis=1)
    with jax.named_scope("grad_normed_line"):
        grad_unit = line_scatter(grad_proj[:HALF], grad_proj[HALF:], lambda v: dot_nt(v, qkv_full))
        d_tokens = grad_middle + unit_norm_back(inputs, grad_unit)
    with jax.named_scope("grad_out_plane"):
        grad_out = dot_tn(heads_out, jnp.concatenate(grad_attn)).astype(BF)
        grad_out = turned(plane_scatter(grad_out, 1).astype(BF)).astype(F32)
    with jax.named_scope("grad_qkv_plane"):
        grad_qkv = dot_tn(jnp.concatenate(normed), grad_proj).astype(BF)
        grad_qkv = plane_scatter(grad_qkv, 0)
    with jax.named_scope("grad_qkv_line"):
        grad_qkv = line_exchange(grad_qkv.astype(BF).reshape(8, 32, -1)).astype(F32)
        q_part = grad_qkv[:, :, :Q_HERE].transpose(1, 0, 2).reshape(32, D)
        kv_part = grad_qkv[:, :, Q_HERE:].reshape(KV_HEADS, 2, 32, 2, HEAD_DIM).sum(axis=1)
        kv_part = kv_part.transpose(1, 2, 0, 3).reshape(32, 2 * KV_HEADS * HEAD_DIM)
        grad_qkv = jnp.concatenate([q_part, kv_part], axis=1)

    grad_gains = jnp.stack(
        [jnp.sum(qkv_low * grad_qkv, axis=1), jnp.sum(gate_low * grad_gate, axis=1)]
    )
    qkv_new = adam_step(w_qkv, grad_qkv * gain_rows[:, 0:1], m_qkv, v_qkv, RATE_QKV)
    out_new = adam_step(w_out, grad_out, m_out, v_out, RATE_OUT)
    gate_new = adam_step(w_gate_up, grad_gate * gain_rows[:, 1:2], m_gate_up, v_gate_up, RATE_GATE_UP)
    down_new = adam_step(w_down, grad_down, m_down, v_down, RATE_DOWN)
    gains_new = adam_step(gains, grad_gains, m_gains, v_gains, RATE_GAINS)
    return (mixed, d_tokens, *qkv_new, *out_new, *gate_new, *down_new, *gains_new)


def solution(mesh):
    tokens = P(BOTH, None)
    ids = P(BOTH)
    rows = P("shard", None)
    columns = P(None, "shard")
    return jax.shard_map(
        on_device,
        mesh=mesh,
        in_specs=(tokens, tokens, ids, ids, rows, rows, rows, rows, columns)
        + (rows,) * 8
        + (columns,) * 2,
        out_specs=(tokens, tokens) + (rows,) * 12 + (columns,) * 3,
        check_vma=False,
    )
```

```python
import functools

import jax
import jax.numpy as jnp
from jax import lax
from jax.experimental import pallas as pl
from jax.experimental.pallas import tpu as pltpu
from jax.sharding import PartitionSpec as P

HEADS = 32
KV_HEADS = 4
HEAD_DIM = 64
D = 2048
FF = 5632
STEP = 10
ROWS = 128
GROUP = 8
TOK = ROWS * GROUP
HALF = TOK // 2
HEADS_HERE = HEADS // GROUP
Q_HERE = HEADS_HERE * HEAD_DIM
PROJ_HERE = Q_HERE + 2 * HEAD_DIM
FF_HERE = FF // GROUP
FF_MAIN = FF_HERE // 128 * 128
FF_REST = FF_HERE - FF_MAIN
Q_BLOCK = 256
VMEM = 60 * 2**20

EPSILON = 1e-05
BETA_ONE = 0.9
BETA_TWO = 0.95
ADAM_EPSILON = 1e-08
DECAY = 0.1
RATE_QKV = 0.02
RATE_OUT = 0.25
RATE_GATE_UP = 0.02
RATE_DOWN = 0.013
RATE_GAINS = 0.3

BF = jnp.bfloat16
F32 = jnp.float32
BOTH = ("rep", "shard")
LINES = [[8 * b + a for a in range(8)] for b in range(8)]
PLANES = [[8 * b + a for b in range(8)] for a in range(8)]


def index_of(r, y, z, x, c):
    return r * 64 + y * 16 + z * 8 + x * 2 + c


def places():
    return [
        (r, y, z, x, c)
        for r in range(2)
        for y in range(4)
        for z in range(2)
        for x in range(4)
        for c in range(2)
    ]


def come_from(v, y=0, x=0, c=0, zz=0):
    pairs = []
    for r, yy, z, xx, cc in places():
        ring = (2 * r + z + zz) % 4
        source = index_of(ring // 2, (yy + y) % 4, ring % 2, (xx + x) % 4, cc ^ c)
        pairs.append((source, index_of(r, yy, z, xx, cc)))
    return lax.ppermute(v, BOTH, pairs)


def turned(v):
    pairs = [(index_of(r, x, c, y, z), index_of(r, y, z, x, c)) for r, y, z, x, c in places()]
    return lax.ppermute(v, BOTH, pairs)


def dot(left, right):
    return jnp.dot(left, right, preferred_element_type=F32)


def dot_nt(left, right):
    return lax.dot_general(left, right, (((1,), (1,)), ((), ())), preferred_element_type=F32)


def dot_tn(left, right):
    return lax.dot_general(left, right, (((0,), (0,)), ((), ())), preferred_element_type=F32)


def after(v, *events):
    for event in events:
        last = event[(-1,) * event.ndim]
        v = jnp.where(last == last, v, jnp.zeros_like(v))
    return v


def settled(v):
    return lax.optimization_barrier(v)


def halves_gather(v):
    pieces = line_pieces(v)
    near, far = line_halves(v, pieces)
    return near, far, pieces[0]


def line_pieces(v):
    return [come_from(v, x=k) for k in (1, 2, 3)]


def line_halves(v, pieces):
    near = settled(jnp.concatenate([v] + pieces, axis=0))
    return near, come_from(near, c=1)


def plane_exchange(v):
    return lax.all_to_all(v, "shard", 0, 0, tiled=True, axis_index_groups=PLANES)


def plane_spread(v):
    parts = plane_exchange(jnp.broadcast_to(v[None], (8, *v.shape)))
    return parts.reshape(8 * v.shape[0], v.shape[1])


def plane_gather(v):
    return lax.all_gather(v, "shard", axis=0, tiled=True, axis_index_groups=PLANES)


def plane_scatter(v):
    return lax.psum_scatter(
        v, "shard", scatter_dimension=0, tiled=True, axis_index_groups=PLANES
    )


def rep_sum(total):
    return total + come_from(total.astype(BF), zz=2).astype(F32)


def line_exchange(v):
    return lax.all_to_all(v, "shard", 0, 0, tiled=True, axis_index_groups=LINES)


def rate_of(values):
    return lax.rsqrt(jnp.mean(values * values, axis=-1, keepdims=True) + EPSILON)


def unit_norm(values):
    return values * rate_of(values)


def unit_norm_back(values, grad):
    rate = rate_of(values)
    unit = values * rate
    return rate * (grad - unit * jnp.mean(grad * unit, axis=-1, keepdims=True))


def adam_step(weight, grad, first, second, rate):
    first_new = BETA_ONE * first + (1.0 - BETA_ONE) * grad
    second_new = BETA_TWO * second + (1.0 - BETA_TWO) * grad * grad
    first_hat = first_new / (1.0 - BETA_ONE**STEP)
    second_hat = second_new / (1.0 - BETA_TWO**STEP)
    weight_new = weight - rate * (
        first_hat / (jnp.sqrt(second_hat) + ADAM_EPSILON) + DECAY * weight
    )
    return (weight_new, first_new, second_new)


TINY = pl.CostEstimate(flops=1, bytes_accessed=1, transcendentals=0)
ANY = pl.BlockSpec(memory_space=pl.ANY)


def cost(flops):
    return pl.CostEstimate(flops=int(flops), bytes_accessed=1, transcendentals=0)


def core_sum_kernel(near_ref, came_ref, *refs):
    own_ref, *piece_refs = refs[-4:]
    total = near_ref[...].astype(F32) + came_ref[...].astype(F32)
    step = pl.program_id(0)

    @pl.when(step == 0)
    def _():
        own_ref[...] = total

    for k in (1, 2, 3):

        @pl.when(step == k)
        def _(k=k):
            piece_refs[k - 1][...] = total.astype(BF)


def line_scatter(near, far, *events):
    here = pl.BlockSpec((ROWS, D), lambda i: (0, 0))
    own, *pieces = pl.pallas_call(
        core_sum_kernel,
        grid=(4,),
        in_specs=[pl.BlockSpec((ROWS, D), lambda i: (i, 0))] * 2 + [ANY] * len(events),
        out_specs=[here] * 4,
        out_shape=[jax.ShapeDtypeStruct((ROWS, D), F32)]
        + [jax.ShapeDtypeStruct((ROWS, D), BF)] * 3,
        cost_estimate=TINY,
        compiler_params=pltpu.CompilerParams(vmem_limit_bytes=VMEM),
        name="core_sum",
    )(near, come_from(far, c=1), *events)
    return own, [come_from(piece, x=-k) for k, piece in zip((1, 2, 3), pieces)]


def pieces_sum(refs):
    total = refs[0][...]
    for ref in refs[1:4]:
        total = total + ref[...].astype(F32)
    return total


def middle_kernel(*refs):
    tokens_ref, middle_ref, normed_ref = refs[4], refs[-2], refs[-1]
    middle = tokens_ref[...].astype(F32) + pieces_sum(refs)
    middle_ref[...] = middle
    normed_ref[...] = unit_norm(middle).astype(BF)


def middle_back_kernel(*refs):
    middle_ref, cotangent_ref, grad_ref, low_ref = refs[4], refs[5], refs[-2], refs[-1]
    grad = cotangent_ref[...].astype(F32) + unit_norm_back(middle_ref[...], pieces_sum(refs))
    grad_ref[...] = grad
    low_ref[...] = grad.astype(BF)


def tokens_back_kernel(*refs):
    tokens_ref, middle_ref, out_ref = refs[4], refs[5], refs[-1]
    out_ref[...] = middle_ref[...] + unit_norm_back(tokens_ref[...].astype(F32), pieces_sum(refs))


def mixed_kernel(*refs):
    refs[-1][...] = refs[4][...] + pieces_sum(refs)


def row_kernel(kernel, own, pieces, others, outs, events=()):
    count = 1 + len(pieces) + len(others)
    spec = pl.BlockSpec((ROWS, D), lambda: (0, 0))
    return pl.pallas_call(
        kernel,
        in_specs=[spec] * count + [ANY] * len(events),
        out_specs=[spec] * len(outs),
        out_shape=[jax.ShapeDtypeStruct((ROWS, D), t) for t in outs],
        cost_estimate=TINY,
        compiler_params=pltpu.CompilerParams(vmem_limit_bytes=VMEM),
        name=kernel.__name__,
    )(own, *pieces, *others, *events)


def parts_sum_kernel(parts_ref, *refs):
    total = parts_ref[0].astype(F32)
    for k in range(1, parts_ref.shape[0]):
        total = total + parts_ref[k].astype(F32)
    refs[-2][...] = total
    refs[-1][...] = total.astype(BF)


def parts_sum(parts, block, *events):
    n, rows, cols = parts.shape
    out = pl.BlockSpec((block, cols), lambda i: (i, 0))
    return pl.pallas_call(
        parts_sum_kernel,
        grid=(rows // block,),
        in_specs=[pl.BlockSpec((n, block, cols), lambda i: (0, i, 0))] + [ANY] * len(events),
        out_specs=[out] * 2,
        out_shape=[jax.ShapeDtypeStruct((rows, cols), t) for t in (F32, BF)],
        cost_estimate=TINY,
        compiler_params=pltpu.CompilerParams(vmem_limit_bytes=VMEM),
        name="parts_sum",
    )(parts, *events)


def lanes(rows):
    return lax.broadcasted_iota(jnp.int32, (rows, 128), 1)


def rotated(v, cosine, sine, lane):
    partner = jnp.where(lane % HEAD_DIM < HEAD_DIM // 2, pltpu.roll(v, 96, 1), pltpu.roll(v, 32, 1))
    return v * cosine + partner * sine


def split_pair(pair, k_ref, v_ref, lane):
    swapped = pltpu.roll(pair, 64, 1)
    low = lane < HEAD_DIM
    zero = jnp.zeros_like(pair)
    k_ref[0] = jnp.where(low, pair, zero).astype(BF)
    k_ref[1] = jnp.where(low, zero, swapped).astype(BF)
    v_ref[0] = jnp.where(low, swapped, zero).astype(BF)
    v_ref[1] = jnp.where(low, zero, pair).astype(BF)


def barred(column_ref, row_ref):
    same = column_ref[:, 0:1] == row_ref[0:1, :]
    before = row_ref[1:2, :] <= column_ref[:, 1:2]
    return jnp.where(same & before, 0.0, -1e30)


def forward_kernel(*refs):
    near_ref, far_ref, w_qkv_ref, cos_ref, sin_ref, cos_all_ref, sin_all_ref, column_ref, row_ref = refs[:9]
    out_ref, q_ref, kv_ref, total_ref, proj_scr, k_scr, v_scr = refs[-7:]
    lane = lanes(Q_BLOCK)
    step = pl.program_id(0)

    @pl.when(step == 0)
    def _():
        for i in range(TOK // Q_BLOCK):
            ref = near_ref if i * Q_BLOCK < HALF else far_ref
            rows = ref[i * Q_BLOCK % HALF : i * Q_BLOCK % HALF + Q_BLOCK]
            proj_scr[i * Q_BLOCK : (i + 1) * Q_BLOCK] = dot(rows, w_qkv_ref[...])
        wide = lanes(TOK)
        pair = proj_scr[:, Q_HERE:]
        turned_pair = rotated(pair, cos_all_ref[...], sin_all_ref[...], wide)
        pair = jnp.where(wide < HEAD_DIM, turned_pair, pair).astype(BF)
        kv_ref[...] = pair
        split_pair(pair.astype(F32), k_scr, v_scr, wide)

    bar = barred(column_ref, row_ref)
    totals = jnp.zeros((Q_BLOCK, 128), F32)
    here = pl.ds(pl.multiple_of(step * Q_BLOCK, Q_BLOCK), Q_BLOCK)
    for chunk in range(HEADS_HERE // 2):
        span = slice(128 * chunk, 128 * (chunk + 1))
        queries = rotated(proj_scr[here, span], cos_ref[...], sin_ref[...], lane).astype(BF)
        queries = (queries.astype(F32) * HEAD_DIM**-0.5).astype(BF)
        q_ref[:, span] = queries
        out = jnp.zeros((Q_BLOCK, 128), F32)
        for side in range(2):
            scores = dot_nt(queries, k_scr[side]) + bar
            peak = jnp.max(scores, axis=1, keepdims=True)
            expo = jnp.exp(scores - peak)
            total = jnp.sum(expo, axis=1, keepdims=True)
            probs = (expo * (1.0 / total)).astype(BF)
            out = out + dot(probs, v_scr[side])
            totals = jnp.where(lane == 2 * chunk + side, peak + jnp.log(total), totals)
        out_ref[:, span] = out.astype(BF)
    total_ref[...] = totals


def backward_kernel(*refs):
    near_ref, far_ref, w_out_ref, q_ref, kv_ref, total_ref, cos_ref, sin_ref, cos_all_ref, sin_all_ref = refs[:10]
    column_ref, row_ref = refs[10:12]
    dproj_ref, do_scr, k_scr, v_scr, dk_scr, dv_scr = refs[-6:]
    lane = lanes(Q_BLOCK)
    step = pl.program_id(0)

    @pl.when(step == 0)
    def _():
        split_pair(kv_ref[...].astype(F32), k_scr, v_scr, lanes(TOK))
        dk_scr[...] = jnp.zeros_like(dk_scr)
        dv_scr[...] = jnp.zeros_like(dv_scr)

    @pl.when(step < HALF // Q_BLOCK)
    def _():
        do_scr[...] = dot_nt(near_ref[...], w_out_ref[...]).astype(BF)

    @pl.when(step >= HALF // Q_BLOCK)
    def _():
        do_scr[...] = dot_nt(far_ref[...], w_out_ref[...]).astype(BF)

    bar = barred(column_ref, row_ref)
    here = pl.ds(pl.multiple_of(step * Q_BLOCK, Q_BLOCK), Q_BLOCK)
    for chunk in range(HEADS_HERE // 2):
        span = slice(128 * chunk, 128 * (chunk + 1))
        queries = q_ref[:, span]
        grads = do_scr[:, span]
        dq = jnp.zeros((Q_BLOCK, 128), F32)
        for side in range(2):
            held = (lane >= HEAD_DIM) == (side == 1)
            head = 2 * chunk + side
            scores = dot_nt(queries, k_scr[side]) + bar
            probs = jnp.exp(scores - total_ref[:, head : head + 1])
            dp = dot_nt(grads, v_scr[side])
            inner = jnp.sum(probs * dp, axis=1, keepdims=True)
            ds = (probs * (dp - inner)).astype(BF)
            dq = dq + dot(ds, k_scr[side])
            dk_scr[...] += dot_tn(ds, jnp.where(held, queries, jnp.zeros_like(queries)))
            dv_scr[...] += dot_tn(
                probs.astype(BF), jnp.where(held, grads, jnp.zeros_like(grads))
            )
        dq = dq * HEAD_DIM**-0.5
        dproj_ref[here, span] = rotated(dq, cos_ref[...], -sin_ref[...], lane).astype(BF)

    @pl.when(step == pl.num_programs(0) - 1)
    def _():
        wide = lanes(TOK)
        dk = dk_scr[...] + pltpu.roll(dk_scr[...], 64, 1)
        dv = dv_scr[...] + pltpu.roll(dv_scr[...], 64, 1)
        dk = rotated(dk, cos_all_ref[...], -sin_all_ref[...], wide)
        dproj_ref[:, Q_HERE:] = jnp.where(wide < HEAD_DIM, dk, dv).astype(BF)


def blocked(cols):
    return pl.BlockSpec((Q_BLOCK, cols), lambda i: (i, 0))


def whole(rows, cols):
    return pl.BlockSpec((rows, cols), lambda i: (0, 0), pipeline_mode=pl.Buffered(1))


def near_block(cols):
    return pl.BlockSpec((Q_BLOCK, cols), lambda i: (jnp.minimum(i, HALF // Q_BLOCK - 1), 0))


def far_block(cols):
    return pl.BlockSpec((Q_BLOCK, cols), lambda i: (jnp.maximum(i - HALF // Q_BLOCK, 0), 0))


def attend(near, far, w_qkv, cosine, sine, column, row, *events):
    return pl.pallas_call(
        forward_kernel,
        grid=(TOK // Q_BLOCK,),
        in_specs=[
            whole(HALF, D),
            whole(HALF, D),
            whole(D, PROJ_HERE),
            blocked(128),
            blocked(128),
            whole(TOK, 128),
            whole(TOK, 128),
            blocked(2),
            whole(2, TOK),
        ]
        + [ANY] * len(events),
        out_specs=[
            blocked(Q_HERE),
            blocked(Q_HERE),
            pl.BlockSpec((TOK, 128), lambda i: (0, 0)),
            blocked(128),
        ],
        out_shape=[
            jax.ShapeDtypeStruct((TOK, Q_HERE), BF),
            jax.ShapeDtypeStruct((TOK, Q_HERE), BF),
            jax.ShapeDtypeStruct((TOK, 128), BF),
            jax.ShapeDtypeStruct((TOK, 128), F32),
        ],
        scratch_shapes=[
            pltpu.VMEM((TOK, PROJ_HERE), F32),
            pltpu.VMEM((2, TOK, 128), BF),
            pltpu.VMEM((2, TOK, 128), BF),
        ],
        compiler_params=pltpu.CompilerParams(vmem_limit_bytes=VMEM),
        cost_estimate=cost(30e9),
        name="attention_forward",
    )(near, far, w_qkv, cosine, sine, cosine, sine, column, row, *events)


def attend_back(near, far, w_out, queries, pair, totals, cosine, sine, column, row, *events):
    return pl.pallas_call(
        backward_kernel,
        grid=(TOK // Q_BLOCK,),
        in_specs=[
            near_block(D),
            far_block(D),
            whole(Q_HERE, D),
            blocked(Q_HERE),
            whole(TOK, 128),
            blocked(128),
            blocked(128),
            blocked(128),
            whole(TOK, 128),
            whole(TOK, 128),
            blocked(2),
            whole(2, TOK),
        ]
        + [ANY] * len(events),
        out_specs=pl.BlockSpec((TOK, PROJ_HERE), lambda i: (0, 0)),
        out_shape=jax.ShapeDtypeStruct((TOK, PROJ_HERE), BF),
        scratch_shapes=[
            pltpu.VMEM((Q_BLOCK, Q_HERE), BF),
            pltpu.VMEM((2, TOK, 128), BF),
            pltpu.VMEM((2, TOK, 128), BF),
            pltpu.VMEM((TOK, 128), F32),
            pltpu.VMEM((TOK, 128), F32),
        ],
        compiler_params=pltpu.CompilerParams(vmem_limit_bytes=VMEM),
        cost_estimate=cost(30e9),
        name="attention_backward",
    )(near, far, w_out, queries, pair, totals, cosine, sine, cosine, sine, column, row, *events)


def line_dot_kernel(*refs, turned_weight):
    rows_ref, w_ref, near_ref, far_ref = refs[0], refs[1], refs[-2], refs[-1]
    product = dot_nt if turned_weight else dot
    part = product(rows_ref[...], w_ref[...]).astype(BF)

    @pl.when(pl.program_id(0) < HALF // Q_BLOCK)
    def _():
        near_ref[...] = part

    @pl.when(pl.program_id(0) >= HALF // Q_BLOCK)
    def _():
        far_ref[...] = part


def line_dot(rows, weight, turned_weight, *events):
    return pl.pallas_call(
        functools.partial(line_dot_kernel, turned_weight=turned_weight),
        grid=(TOK // Q_BLOCK,),
        in_specs=[blocked(rows.shape[1]), whole(*weight.shape)] + [ANY] * len(events),
        out_specs=[near_block(D), far_block(D)],
        out_shape=[jax.ShapeDtypeStruct((HALF, D), BF)] * 2,
        compiler_params=pltpu.CompilerParams(vmem_limit_bytes=VMEM),
        cost_estimate=TINY,
        name="line_dot",
    )(rows, weight, *events)


def feed_forward_kernel(
    near_ref, far_ref, grads_near_ref, grads_far_ref, gate_ref, down_ref,
    hid_near_ref, hid_far_ref, dgu_near_ref, dgu_far_ref, dn_near_ref, dn_far_ref, mix_near_ref, mix_far_ref,
):
    rows = jnp.concatenate([near_ref[...], far_ref[...]], axis=0)
    grads = jnp.concatenate([grads_near_ref[...], grads_far_ref[...]], axis=0)
    gate_up = dot(rows, gate_ref[...])
    dhid = dot_nt(grads, down_ref[...])

    def unit(gate, up, grad):
        sig = 1.0 / (1.0 + jnp.exp(-gate))
        act = gate * sig
        return act * up, grad * up * (sig + act * (1.0 - sig)), grad * act

    hid, dgate, dup = unit(
        gate_up[:, :FF_MAIN], gate_up[:, FF_MAIN : 2 * FF_MAIN], dhid[:, :FF_MAIN]
    )
    last = gate_up[:, 2 * FF_MAIN :]
    grad = jnp.concatenate([dhid[:, FF_MAIN:], dhid[:, FF_MAIN:]], axis=1)
    hid_last, dgate_last, dup_last = unit(last, pltpu.roll(last, FF_REST, 1), grad)
    low = lax.broadcasted_iota(jnp.int32, last.shape, 1) < FF_REST
    last = jnp.where(low, dgate_last, pltpu.roll(dup_last, FF_REST, 1))
    hid = hid.astype(BF)
    hid_last = hid_last[:, :FF_REST].astype(BF)
    hid_near_ref[:, :FF_MAIN] = hid[:ROWS]
    hid_near_ref[:, FF_MAIN:] = hid_last[:ROWS]
    hid_far_ref[:, :FF_MAIN] = hid[ROWS:]
    hid_far_ref[:, FF_MAIN:] = hid_last[ROWS:]
    dgu = jnp.concatenate([dgate.astype(BF), dup.astype(BF), last.astype(BF)], axis=1)
    dgu_near_ref[...] = dgu[:ROWS]
    dgu_far_ref[...] = dgu[ROWS:]
    dn = dot_nt(dgu, gate_ref[...]).astype(BF)
    dn_near_ref[...] = dn[:ROWS]
    dn_far_ref[...] = dn[ROWS:]
    mix = dot(jnp.concatenate([hid, hid_last], axis=1), down_ref[...]).astype(BF)
    mix_near_ref[...] = mix[:ROWS]
    mix_far_ref[...] = mix[ROWS:]


def feed_forward(near, far, grads_near, grads_far, gate_full, down_full):
    def side(cols):
        return pl.BlockSpec((ROWS, cols), lambda i: (i, 0))

    outs = (FF_HERE, FF_HERE, 2 * FF_HERE, 2 * FF_HERE, D, D, D, D)
    return pl.pallas_call(
        feed_forward_kernel,
        grid=(4,),
        in_specs=[side(D)] * 4 + [whole(D, 2 * FF_HERE), whole(FF_HERE, D)],
        out_specs=[side(c) for c in outs],
        out_shape=[jax.ShapeDtypeStruct((HALF, c), BF) for c in outs],
        compiler_params=pltpu.CompilerParams(vmem_limit_bytes=VMEM),
        cost_estimate=cost(30e9),
        name="feed_forward",
    )(near, far, grads_near, grads_far, gate_full, down_full)


def weight_grad_kernel(near_ref, far_ref, g_near_ref, g_far_ref, *refs):
    grad = dot_tn(near_ref[...], g_near_ref[...]) + dot_tn(far_ref[...], g_far_ref[...])
    refs[-1][...] = grad.astype(BF)


def weight_grad(near, far, grads_near, grads_far, far_block_index, block, flops, *events):
    deep, cols = near.shape[1], grads_near.shape[1]
    if block == cols:
        grid = deep // 256
        rows = pl.BlockSpec((HALF, 256), lambda i: (0, i))
        grads = [pl.BlockSpec((HALF, cols), lambda i, k=k: (k, 0)) for k in (0, far_block_index)]
        out = pl.BlockSpec((256, cols), lambda i: (i, 0))
    else:
        grid = cols // block
        rows = pl.BlockSpec((HALF, deep), lambda i: (0, 0))
        grads = [pl.BlockSpec((HALF, block), lambda i, k=k: (k, i)) for k in (0, far_block_index)]
        out = pl.BlockSpec((deep, block), lambda i: (0, i))
    return pl.pallas_call(
        weight_grad_kernel,
        grid=(grid,),
        in_specs=[rows, rows, *grads] + [ANY] * len(events),
        out_specs=out,
        out_shape=jax.ShapeDtypeStruct((deep, cols), BF),
        compiler_params=pltpu.CompilerParams(vmem_limit_bytes=VMEM),
        cost_estimate=cost(flops),
        name="weight_grad",
    )(near, far, grads_near, grads_far, *events)


def small_rows(segment_ids, position_ids):
    parts = [position_ids // 32, position_ids % 32, segment_ids // 128, segment_ids % 128]
    flat = jnp.concatenate([p.astype(BF) for p in parts])
    return jnp.pad(flat[None], ((0, 7), (0, PROJ_HERE + 2 * FF_HERE - 512)))


def small_read(rows):
    s = lax.axis_index("shard")
    x, c = (s // 2) % 4, s % 2
    line = rows[:, 0, :512].reshape(4, 2, 4, 128).astype(F32)
    line = lax.dynamic_slice(jnp.concatenate([line, line], axis=0), (x, 0, 0, 0), (4, 2, 4, 128))
    line = jnp.where(c == 0, line, line[:, ::-1]).transpose(1, 0, 2, 3).reshape(8, 4, 128)
    position = (line[:, 0] * 32.0 + line[:, 1]).reshape(TOK)
    segment = (line[:, 2] * 128.0 + line[:, 3]).reshape(TOK)
    return position, segment


def on_device(
    tokens,
    cotangent,
    segment_ids,
    position_ids,
    w_qkv,
    w_out,
    w_gate_up,
    w_down,
    gains,
    m_qkv,
    v_qkv,
    m_out,
    v_out,
    m_gate_up,
    v_gate_up,
    m_down,
    v_down,
    m_gains,
    v_gains,
):
    gain_rows = gains.astype(BF).astype(F32).T
    qkv_low = w_qkv.astype(BF).astype(F32)
    gate_low = w_gate_up.astype(BF).astype(F32)

    with jax.named_scope("qkv_weights_line"):
        low = (qkv_low * gain_rows[:, 0:1]).astype(BF)
        q_cols = low[:, :D].reshape(32, 8, Q_HERE)
        kv_cols = low[:, D:].reshape(32, 2, KV_HEADS, HEAD_DIM).transpose(0, 2, 1, 3)
        kv_cols = jnp.repeat(kv_cols.reshape(32, KV_HEADS, 2 * HEAD_DIM), 2, axis=1)
        qkv_cut = jnp.concatenate([q_cols, kv_cols], axis=2).transpose(1, 0, 2)
    with jax.named_scope("gate_weights_line"):
        low = (gate_low * gain_rows[:, 1:2]).astype(BF)
        low = low.reshape(32, 2, 8, FF_HERE)
        gate_cut = jnp.concatenate(
            [low[:, 0, :, :FF_MAIN], low[:, 1, :, :FF_MAIN], low[:, 0, :, FF_MAIN:], low[:, 1, :, FF_MAIN:]],
            axis=2,
        )
        both = jnp.concatenate([qkv_cut, gate_cut.transpose(1, 0, 2)], axis=2)
        small = small_rows(segment_ids, position_ids)
        small = jnp.broadcast_to(small[None], (8, *small.shape))
        both = line_exchange(jnp.concatenate([both, small], axis=1))
        positions, segments = small_read(both[:, 32:])
        qkv_line = both[:, :32, :PROJ_HERE].reshape(256, PROJ_HERE)
        gate_line = both[:, :32, PROJ_HERE:].reshape(256, 2 * FF_HERE)
    with jax.named_scope("gate_weights_plane"):
        gate_full = plane_gather(gate_line)
    with jax.named_scope("qkv_weights_plane"):
        qkv_full = plane_spread(qkv_line)
    with jax.named_scope("normed_line"):
        normed = unit_norm(tokens.astype(F32)).astype(BF)
        pieces = line_pieces(normed)
        near, far = line_halves(normed, pieces)
    with jax.named_scope("cotangent_line"):
        cot_pieces = line_pieces(after(cotangent, near))
    with jax.named_scope("out_turn"):
        out_turned = turned(w_out.astype(BF))
    with jax.named_scope("down_turn"):
        down_turned = turned(after(w_down.astype(BF), near))
    with jax.named_scope("out_weights_plane"):
        out_full = plane_spread(after(out_turned, qkv_full))
    with jax.named_scope("down_weights_plane"):
        down_full = plane_spread(after(down_turned, out_full))

    freqs = 10000.0 ** (-jnp.arange(HEAD_DIM // 2).astype(F32) * 2.0 / HEAD_DIM)
    angles = positions[:, None] * freqs[None, :]
    cosine = jnp.tile(jnp.cos(angles), (1, 4))
    sine = jnp.sin(angles)
    sine = jnp.concatenate([-sine, sine, -sine, sine], axis=1)
    row = jnp.stack([segments, positions])
    column = row.T
    heads_out, queries, pair, totals = attend(
        near, far, qkv_full, cosine, sine, column, row, *cot_pieces
    )
    with jax.named_scope("cotangent_line"):
        cot_near, cot_far = line_halves(after(cotangent, heads_out), cot_pieces)
    with jax.named_scope("heads_out_line"):
        own, pieces = line_scatter(*line_dot(heads_out, out_full, False, cot_near))
        middle, normed_two = row_kernel(
            middle_kernel, own, pieces, [tokens], [F32, BF], (cot_far, down_full)
        )

    with jax.named_scope("normed_two_line"):
        near_two, far_two = line_halves(normed_two, line_pieces(normed_two))
    hid_near, hid_far, dgu_near, dgu_far, dn_near, dn_far, mix_near, mix_far = feed_forward(
        near_two, far_two, cot_near, cot_far, gate_full, down_full
    )
    with jax.named_scope("grad_gate_plane"):
        grad_gate = weight_grad(near_two, far_two, dgu_near, dgu_far, 0, 2 * FF_HERE, 15e9)
        gate_owned = plane_scatter(grad_gate)
    with jax.named_scope("grad_normed_two_line"):
        own, pieces = line_scatter(dn_near, dn_far, grad_gate)
    with jax.named_scope("grad_down_plane"):
        grad_down = weight_grad(hid_near, hid_far, cot_near, cot_far, 0, 512, 1, own)
        down_parts = plane_exchange(grad_down.reshape(8, 88, D))
    with jax.named_scope("mixed_line"):
        mixed_own, mixed_pieces = line_scatter(mix_near, mix_far)
    with jax.named_scope("grad_normed_two_line"):
        grad_middle, grad_attn = row_kernel(
            middle_back_kernel, own, pieces, [middle, cotangent], [F32, BF], (grad_down, mixed_own)
        )
    with jax.named_scope("grad_attn_line"):
        pieces = line_pieces(grad_attn)
        attn_near, attn_far = line_halves(grad_attn, pieces)
    grad_proj = attend_back(
        attn_near, attn_far, out_full, queries, pair, totals, cosine, sine, column, row,
        mixed_own,
    )
    with jax.named_scope("mixed_line"):
        (mixed,) = row_kernel(mixed_kernel, mixed_own, mixed_pieces, [middle], [F32], (grad_proj,))
    with jax.named_scope("grad_qkv"):
        grad_qkv_local = weight_grad(
            near, far, grad_proj, grad_proj, 1, PROJ_HERE, 5e9, mixed
        )
        qkv_parts = plane_exchange(grad_qkv_local.reshape(8, 256, PROJ_HERE))
    with jax.named_scope("grad_out_plane"):
        grad_out = weight_grad(heads_out[:HALF], heads_out[HALF:], attn_near, attn_far, 0, 512, 1, grad_qkv_local)
    with jax.named_scope("grad_normed_line"):
        own, pieces = line_scatter(*line_dot(grad_proj, qkv_full, True, grad_out, down_parts))
    with jax.named_scope("grad_down_rep"):
        down_owned, down_low = parts_sum(down_parts, 88, pieces[0])
        down_sum = down_owned + come_from(down_low, zz=2).astype(F32)
        grad_down = turned(after(down_sum.astype(BF), pieces[0])).astype(F32)
    with jax.named_scope("grad_gate_rep"):
        gate_low_sum = after(gate_owned, pieces[0])
        gate_from_rep = come_from(gate_low_sum, zz=2)
        gate_sum = gate_low_sum.astype(F32) + gate_from_rep.astype(F32)
    with jax.named_scope("grad_normed_line"):
        (d_tokens,) = row_kernel(
            tokens_back_kernel, own, pieces, [tokens, grad_middle], [F32]
        )
    with jax.named_scope("grad_out_rep"):
        out_parts = plane_exchange(after(grad_out.reshape(8, 32, D), qkv_parts, own))
        out_owned, out_low = parts_sum(out_parts, 32, gate_from_rep)
        out_sum = out_owned + come_from(out_low, zz=2).astype(F32)
        grad_out = turned(out_sum.astype(BF)).astype(F32)
    with jax.named_scope("grad_gate_line"):
        gate_sum = after(gate_sum.astype(BF), pieces[0])
        parts = line_exchange(gate_sum.reshape(8, 32, 2 * FF_HERE)).astype(F32)
        main, rest = 2 * FF_MAIN, 2 * FF_MAIN + FF_REST
        grad_gate = jnp.stack(
            [
                jnp.concatenate([parts[:, :, :FF_MAIN], parts[:, :, main:rest]], axis=2),
                jnp.concatenate([parts[:, :, FF_MAIN:main], parts[:, :, rest:]], axis=2),
            ]
        )
        grad_gate = grad_gate.transpose(2, 0, 1, 3).reshape(32, 2 * FF)
    with jax.named_scope("grad_qkv"):
        qkv_sum, qkv_low_sum = parts_sum(qkv_parts, 256, pieces[0])
        qkv_sum = qkv_sum + come_from(qkv_low_sum, zz=2).astype(F32)
        parts = line_exchange(qkv_sum.astype(BF).reshape(8, 32, PROJ_HERE)).astype(F32)
        q_part = parts[:, :, :Q_HERE].transpose(1, 0, 2).reshape(32, D)
        kv_part = parts[:, :, Q_HERE:].reshape(KV_HEADS, 2, 32, 2, HEAD_DIM).sum(axis=1)
        kv_part = kv_part.transpose(1, 2, 0, 3).reshape(32, 2 * KV_HEADS * HEAD_DIM)
        grad_qkv = jnp.concatenate([q_part, kv_part], axis=1)

    grad_gains = jnp.stack(
        [jnp.sum(qkv_low * grad_qkv, axis=1), jnp.sum(gate_low * grad_gate, axis=1)]
    )
    qkv_new = adam_step(w_qkv, grad_qkv * gain_rows[:, 0:1], m_qkv, v_qkv, RATE_QKV)
    out_new = adam_step(w_out, grad_out, m_out, v_out, RATE_OUT)
    gate_new = adam_step(w_gate_up, grad_gate * gain_rows[:, 1:2], m_gate_up, v_gate_up, RATE_GATE_UP)
    down_new = adam_step(w_down, grad_down, m_down, v_down, RATE_DOWN)
    gains_new = adam_step(gains, grad_gains, m_gains, v_gains, RATE_GAINS)
    return (mixed, d_tokens, *qkv_new, *out_new, *gate_new, *down_new, *gains_new)


def solution(mesh):
    tokens = P(BOTH, None)
    ids = P(BOTH)
    rows = P("shard", None)
    columns = P(None, "shard")
    return jax.shard_map(
        on_device,
        mesh=mesh,
        in_specs=(tokens, tokens, ids, ids, rows, rows, rows, rows, columns)
        + (rows,) * 8
        + (columns,) * 2,
        out_specs=(tokens, tokens) + (rows,) * 12 + (columns,) * 3,
        check_vma=False,
    )
```

```python
import functools

import jax
import jax.numpy as jnp
from jax import lax
from jax.experimental import pallas as pl
from jax.experimental.pallas import tpu as pltpu
from jax.sharding import PartitionSpec as P

HEADS = 32
KV_HEADS = 4
HEAD_DIM = 64
D = 2048
FF = 5632
STEP = 10
ROWS = 128
GROUP = 8
TOK = ROWS * GROUP
HALF = TOK // 2
HEADS_HERE = HEADS // GROUP
Q_HERE = HEADS_HERE * HEAD_DIM
PROJ_HERE = Q_HERE + 2 * HEAD_DIM
FF_HERE = FF // GROUP
FF_MAIN = FF_HERE // 128 * 128
FF_REST = FF_HERE - FF_MAIN
Q_BLOCK = 256
VMEM = 60 * 2**20

EPSILON = 1e-05
BETA_ONE = 0.9
BETA_TWO = 0.95
ADAM_EPSILON = 1e-08
DECAY = 0.1
RATE_QKV = 0.02
RATE_OUT = 0.25
RATE_GATE_UP = 0.02
RATE_DOWN = 0.013
RATE_GAINS = 0.3

BF = jnp.bfloat16
F32 = jnp.float32
BOTH = ("rep", "shard")
LINES = [[8 * b + a for a in range(8)] for b in range(8)]
PLANES = [[8 * b + a for b in range(8)] for a in range(8)]


def index_of(r, y, z, x, c):
    return r * 64 + y * 16 + z * 8 + x * 2 + c


def places():
    return [
        (r, y, z, x, c)
        for r in range(2)
        for y in range(4)
        for z in range(2)
        for x in range(4)
        for c in range(2)
    ]


def come_from(v, y=0, x=0, c=0, zz=0):
    pairs = []
    for r, yy, z, xx, cc in places():
        ring = (2 * r + z + zz) % 4
        source = index_of(ring // 2, (yy + y) % 4, ring % 2, (xx + x) % 4, cc ^ c)
        pairs.append((source, index_of(r, yy, z, xx, cc)))
    return lax.ppermute(v, BOTH, pairs)


def turned(v):
    pairs = [(index_of(r, x, c, y, z), index_of(r, y, z, x, c)) for r, y, z, x, c in places()]
    return lax.ppermute(v, BOTH, pairs)


def dot(left, right):
    return jnp.dot(left, right, preferred_element_type=F32)


def dot_nt(left, right):
    return lax.dot_general(left, right, (((1,), (1,)), ((), ())), preferred_element_type=F32)


def dot_tn(left, right):
    return lax.dot_general(left, right, (((0,), (0,)), ((), ())), preferred_element_type=F32)


def after(v, *events):
    for event in events:
        last = event[(-1,) * event.ndim]
        v = jnp.where(last == last, v, jnp.zeros_like(v))
    return v


def settled(v):
    return lax.optimization_barrier(v)


def halves_gather(v):
    pieces = line_pieces(v)
    near, far = line_halves(v, pieces)
    return near, far, pieces[0]


def line_pieces(v):
    return [come_from(v, x=k) for k in (1, 2, 3)]


def line_halves(v, pieces):
    near = settled(jnp.concatenate([v] + pieces, axis=0))
    return near, come_from(near, c=1)


def plane_exchange(v):
    return lax.all_to_all(v, "shard", 0, 0, tiled=True, axis_index_groups=PLANES)


def plane_spread(v):
    parts = plane_exchange(jnp.broadcast_to(v[None], (8, *v.shape)))
    return parts.reshape(8 * v.shape[0], v.shape[1])


def plane_gather(v):
    return lax.all_gather(v, "shard", axis=0, tiled=True, axis_index_groups=PLANES)


def plane_scatter(v):
    return lax.psum_scatter(
        v, "shard", scatter_dimension=0, tiled=True, axis_index_groups=PLANES
    )


def rep_sum(total):
    return total + come_from(total.astype(BF), zz=2).astype(F32)


def line_exchange(v):
    return lax.all_to_all(v, "shard", 0, 0, tiled=True, axis_index_groups=LINES)


def rate_of(values):
    return lax.rsqrt(jnp.mean(values * values, axis=-1, keepdims=True) + EPSILON)


def unit_norm(values):
    return values * rate_of(values)


def unit_norm_back(values, grad):
    rate = rate_of(values)
    unit = values * rate
    return rate * (grad - unit * jnp.mean(grad * unit, axis=-1, keepdims=True))


def adam_step(weight, grad, first, second, rate):
    first_new = BETA_ONE * first + (1.0 - BETA_ONE) * grad
    second_new = BETA_TWO * second + (1.0 - BETA_TWO) * grad * grad
    first_hat = first_new / (1.0 - BETA_ONE**STEP)
    second_hat = second_new / (1.0 - BETA_TWO**STEP)
    weight_new = weight - rate * (
        first_hat / (jnp.sqrt(second_hat) + ADAM_EPSILON) + DECAY * weight
    )
    return (weight_new, first_new, second_new)


TINY = pl.CostEstimate(flops=1, bytes_accessed=1, transcendentals=0)
ANY = pl.BlockSpec(memory_space=pl.ANY)


def cost(flops):
    return pl.CostEstimate(flops=int(flops), bytes_accessed=1, transcendentals=0)


def core_sum_kernel(near_ref, came_ref, *refs):
    own_ref, *piece_refs = refs[-4:]
    total = near_ref[...].astype(F32) + came_ref[...].astype(F32)
    step = pl.program_id(0)

    @pl.when(step == 0)
    def _():
        own_ref[...] = total

    for k in (1, 2, 3):

        @pl.when(step == k)
        def _(k=k):
            piece_refs[k - 1][...] = total.astype(BF)


def line_scatter(near, far, *events):
    here = pl.BlockSpec((ROWS, D), lambda i: (0, 0))
    own, *pieces = pl.pallas_call(
        core_sum_kernel,
        grid=(4,),
        in_specs=[pl.BlockSpec((ROWS, D), lambda i: (i, 0))] * 2 + [ANY] * len(events),
        out_specs=[here] * 4,
        out_shape=[jax.ShapeDtypeStruct((ROWS, D), F32)]
        + [jax.ShapeDtypeStruct((ROWS, D), BF)] * 3,
        cost_estimate=TINY,
        compiler_params=pltpu.CompilerParams(vmem_limit_bytes=VMEM),
        name="core_sum",
    )(near, come_from(far, c=1), *events)
    return own, [come_from(piece, x=-k) for k, piece in zip((1, 2, 3), pieces)]


def pieces_sum(refs):
    total = refs[0][...]
    for ref in refs[1:4]:
        total = total + ref[...].astype(F32)
    return total


def middle_kernel(*refs):
    tokens_ref, middle_ref, normed_ref = refs[4], refs[-2], refs[-1]
    middle = tokens_ref[...].astype(F32) + pieces_sum(refs)
    middle_ref[...] = middle
    normed_ref[...] = unit_norm(middle).astype(BF)


def middle_back_kernel(*refs):
    middle_ref, cotangent_ref, grad_ref, low_ref = refs[4], refs[5], refs[-2], refs[-1]
    grad = cotangent_ref[...].astype(F32) + unit_norm_back(middle_ref[...], pieces_sum(refs))
    grad_ref[...] = grad
    low_ref[...] = grad.astype(BF)


def tokens_back_kernel(*refs):
    tokens_ref, middle_ref, out_ref = refs[4], refs[5], refs[-1]
    out_ref[...] = middle_ref[...] + unit_norm_back(tokens_ref[...].astype(F32), pieces_sum(refs))


def mixed_kernel(*refs):
    refs[-1][...] = refs[4][...] + pieces_sum(refs)


def row_kernel(kernel, own, pieces, others, outs, events=()):
    count = 1 + len(pieces) + len(others)
    spec = pl.BlockSpec((ROWS, D), lambda: (0, 0))
    return pl.pallas_call(
        kernel,
        in_specs=[spec] * count + [ANY] * len(events),
        out_specs=[spec] * len(outs),
        out_shape=[jax.ShapeDtypeStruct((ROWS, D), t) for t in outs],
        cost_estimate=TINY,
        compiler_params=pltpu.CompilerParams(vmem_limit_bytes=VMEM),
        name=kernel.__name__,
    )(own, *pieces, *others, *events)


def parts_sum_kernel(parts_ref, *refs):
    total = parts_ref[0].astype(F32)
    for k in range(1, parts_ref.shape[0]):
        total = total + parts_ref[k].astype(F32)
    refs[-2][...] = total
    refs[-1][...] = total.astype(BF)


def parts_sum(parts, block, *events):
    n, rows, cols = parts.shape
    out = pl.BlockSpec((block, cols), lambda i: (i, 0))
    return pl.pallas_call(
        parts_sum_kernel,
        grid=(rows // block,),
        in_specs=[pl.BlockSpec((n, block, cols), lambda i: (0, i, 0))] + [ANY] * len(events),
        out_specs=[out] * 2,
        out_shape=[jax.ShapeDtypeStruct((rows, cols), t) for t in (F32, BF)],
        cost_estimate=TINY,
        compiler_params=pltpu.CompilerParams(vmem_limit_bytes=VMEM),
        name="parts_sum",
    )(parts, *events)


def lanes(rows):
    return lax.broadcasted_iota(jnp.int32, (rows, 128), 1)


def rotated(v, cosine, sine, lane):
    partner = jnp.where(lane % HEAD_DIM < HEAD_DIM // 2, pltpu.roll(v, 96, 1), pltpu.roll(v, 32, 1))
    return v * cosine + partner * sine


def split_pair(pair, k_ref, v_ref, lane):
    swapped = pltpu.roll(pair, 64, 1)
    low = lane < HEAD_DIM
    zero = jnp.zeros_like(pair)
    k_ref[0] = jnp.where(low, pair, zero).astype(BF)
    k_ref[1] = jnp.where(low, zero, swapped).astype(BF)
    v_ref[0] = jnp.where(low, swapped, zero).astype(BF)
    v_ref[1] = jnp.where(low, zero, pair).astype(BF)


def barred(column_ref, row_ref):
    same = column_ref[:, 0:1] == row_ref[0:1, :]
    before = row_ref[1:2, :] <= column_ref[:, 1:2]
    return jnp.where(same & before, 0.0, -1e30)


def forward_kernel(*refs):
    near_ref, far_ref, w_qkv_ref, cos_ref, sin_ref, cos_all_ref, sin_all_ref, column_ref, row_ref = refs[:9]
    out_ref, q_ref, kv_ref, total_ref, proj_scr, k_scr, v_scr = refs[-7:]
    lane = lanes(Q_BLOCK)
    step = pl.program_id(0)

    @pl.when(step == 0)
    def _():
        for i in range(TOK // Q_BLOCK):
            ref = near_ref if i * Q_BLOCK < HALF else far_ref
            rows = ref[i * Q_BLOCK % HALF : i * Q_BLOCK % HALF + Q_BLOCK]
            proj_scr[i * Q_BLOCK : (i + 1) * Q_BLOCK] = dot(rows, w_qkv_ref[...])
        wide = lanes(TOK)
        pair = proj_scr[:, Q_HERE:]
        turned_pair = rotated(pair, cos_all_ref[...], sin_all_ref[...], wide)
        pair = jnp.where(wide < HEAD_DIM, turned_pair, pair).astype(BF)
        kv_ref[...] = pair
        split_pair(pair.astype(F32), k_scr, v_scr, wide)

    bar = barred(column_ref, row_ref)
    totals = jnp.zeros((Q_BLOCK, 128), F32)
    here = pl.ds(pl.multiple_of(step * Q_BLOCK, Q_BLOCK), Q_BLOCK)
    for chunk in range(HEADS_HERE // 2):
        span = slice(128 * chunk, 128 * (chunk + 1))
        queries = rotated(proj_scr[here, span], cos_ref[...], sin_ref[...], lane).astype(BF)
        queries = (queries.astype(F32) * HEAD_DIM**-0.5).astype(BF)
        q_ref[:, span] = queries
        out = jnp.zeros((Q_BLOCK, 128), F32)
        for side in range(2):
            scores = dot_nt(queries, k_scr[side]) + bar
            peak = jnp.max(scores, axis=1, keepdims=True)
            expo = jnp.exp(scores - peak)
            total = jnp.sum(expo, axis=1, keepdims=True)
            probs = (expo * (1.0 / total)).astype(BF)
            out = out + dot(probs, v_scr[side])
            totals = jnp.where(lane == 2 * chunk + side, peak + jnp.log(total), totals)
        out_ref[:, span] = out.astype(BF)
    total_ref[...] = totals


def backward_kernel(*refs):
    near_ref, far_ref, w_out_ref, q_ref, kv_ref, total_ref, cos_ref, sin_ref, cos_all_ref, sin_all_ref = refs[:10]
    column_ref, row_ref = refs[10:12]
    dproj_ref, do_scr, k_scr, v_scr, dk_scr, dv_scr = refs[-6:]
    lane = lanes(Q_BLOCK)
    step = pl.program_id(0)

    @pl.when(step == 0)
    def _():
        split_pair(kv_ref[...].astype(F32), k_scr, v_scr, lanes(TOK))
        dk_scr[...] = jnp.zeros_like(dk_scr)
        dv_scr[...] = jnp.zeros_like(dv_scr)

    @pl.when(step < HALF // Q_BLOCK)
    def _():
        do_scr[...] = dot_nt(near_ref[...], w_out_ref[...]).astype(BF)

    @pl.when(step >= HALF // Q_BLOCK)
    def _():
        do_scr[...] = dot_nt(far_ref[...], w_out_ref[...]).astype(BF)

    bar = barred(column_ref, row_ref)
    here = pl.ds(pl.multiple_of(step * Q_BLOCK, Q_BLOCK), Q_BLOCK)
    for chunk in range(HEADS_HERE // 2):
        span = slice(128 * chunk, 128 * (chunk + 1))
        queries = q_ref[:, span]
        grads = do_scr[:, span]
        dq = jnp.zeros((Q_BLOCK, 128), F32)
        for side in range(2):
            held = (lane >= HEAD_DIM) == (side == 1)
            head = 2 * chunk + side
            scores = dot_nt(queries, k_scr[side]) + bar
            probs = jnp.exp(scores - total_ref[:, head : head + 1])
            dp = dot_nt(grads, v_scr[side])
            inner = jnp.sum(probs * dp, axis=1, keepdims=True)
            ds = (probs * (dp - inner)).astype(BF)
            dq = dq + dot(ds, k_scr[side])
            dk_scr[...] += dot_tn(ds, jnp.where(held, queries, jnp.zeros_like(queries)))
            dv_scr[...] += dot_tn(
                probs.astype(BF), jnp.where(held, grads, jnp.zeros_like(grads))
            )
        dq = dq * HEAD_DIM**-0.5
        dproj_ref[here, span] = rotated(dq, cos_ref[...], -sin_ref[...], lane).astype(BF)

    @pl.when(step == pl.num_programs(0) - 1)
    def _():
        wide = lanes(TOK)
        dk = dk_scr[...] + pltpu.roll(dk_scr[...], 64, 1)
        dv = dv_scr[...] + pltpu.roll(dv_scr[...], 64, 1)
        dk = rotated(dk, cos_all_ref[...], -sin_all_ref[...], wide)
        dproj_ref[:, Q_HERE:] = jnp.where(wide < HEAD_DIM, dk, dv).astype(BF)


def blocked(cols):
    return pl.BlockSpec((Q_BLOCK, cols), lambda i: (i, 0))


def whole(rows, cols):
    return pl.BlockSpec((rows, cols), lambda i: (0, 0), pipeline_mode=pl.Buffered(1))


def near_block(cols):
    return pl.BlockSpec((Q_BLOCK, cols), lambda i: (jnp.minimum(i, HALF // Q_BLOCK - 1), 0))


def far_block(cols):
    return pl.BlockSpec((Q_BLOCK, cols), lambda i: (jnp.maximum(i - HALF // Q_BLOCK, 0), 0))


def attend(near, far, w_qkv, cosine, sine, column, row, *events):
    return pl.pallas_call(
        forward_kernel,
        grid=(TOK // Q_BLOCK,),
        in_specs=[
            whole(HALF, D),
            whole(HALF, D),
            whole(D, PROJ_HERE),
            blocked(128),
            blocked(128),
            whole(TOK, 128),
            whole(TOK, 128),
            blocked(2),
            whole(2, TOK),
        ]
        + [ANY] * len(events),
        out_specs=[
            blocked(Q_HERE),
            blocked(Q_HERE),
            pl.BlockSpec((TOK, 128), lambda i: (0, 0)),
            blocked(128),
        ],
        out_shape=[
            jax.ShapeDtypeStruct((TOK, Q_HERE), BF),
            jax.ShapeDtypeStruct((TOK, Q_HERE), BF),
            jax.ShapeDtypeStruct((TOK, 128), BF),
            jax.ShapeDtypeStruct((TOK, 128), F32),
        ],
        scratch_shapes=[
            pltpu.VMEM((TOK, PROJ_HERE), F32),
            pltpu.VMEM((2, TOK, 128), BF),
            pltpu.VMEM((2, TOK, 128), BF),
        ],
        compiler_params=pltpu.CompilerParams(vmem_limit_bytes=VMEM),
        cost_estimate=cost(30e9),
        name="attention_forward",
    )(near, far, w_qkv, cosine, sine, cosine, sine, column, row, *events)


def attend_back(near, far, w_out, queries, pair, totals, cosine, sine, column, row, *events):
    return pl.pallas_call(
        backward_kernel,
        grid=(TOK // Q_BLOCK,),
        in_specs=[
            near_block(D),
            far_block(D),
            whole(Q_HERE, D),
            blocked(Q_HERE),
            whole(TOK, 128),
            blocked(128),
            blocked(128),
            blocked(128),
            whole(TOK, 128),
            whole(TOK, 128),
            blocked(2),
            whole(2, TOK),
        ]
        + [ANY] * len(events),
        out_specs=pl.BlockSpec((TOK, PROJ_HERE), lambda i: (0, 0)),
        out_shape=jax.ShapeDtypeStruct((TOK, PROJ_HERE), BF),
        scratch_shapes=[
            pltpu.VMEM((Q_BLOCK, Q_HERE), BF),
            pltpu.VMEM((2, TOK, 128), BF),
            pltpu.VMEM((2, TOK, 128), BF),
            pltpu.VMEM((TOK, 128), F32),
            pltpu.VMEM((TOK, 128), F32),
        ],
        compiler_params=pltpu.CompilerParams(vmem_limit_bytes=VMEM),
        cost_estimate=cost(30e9),
        name="attention_backward",
    )(near, far, w_out, queries, pair, totals, cosine, sine, cosine, sine, column, row, *events)


def line_dot_kernel(*refs, turned_weight):
    rows_ref, w_ref, near_ref, far_ref = refs[0], refs[1], refs[-2], refs[-1]
    product = dot_nt if turned_weight else dot
    part = product(rows_ref[...], w_ref[...]).astype(BF)

    @pl.when(pl.program_id(0) < HALF // Q_BLOCK)
    def _():
        near_ref[...] = part

    @pl.when(pl.program_id(0) >= HALF // Q_BLOCK)
    def _():
        far_ref[...] = part


def line_dot(rows, weight, turned_weight, *events):
    return pl.pallas_call(
        functools.partial(line_dot_kernel, turned_weight=turned_weight),
        grid=(TOK // Q_BLOCK,),
        in_specs=[blocked(rows.shape[1]), whole(*weight.shape)] + [ANY] * len(events),
        out_specs=[near_block(D), far_block(D)],
        out_shape=[jax.ShapeDtypeStruct((HALF, D), BF)] * 2,
        compiler_params=pltpu.CompilerParams(vmem_limit_bytes=VMEM),
        cost_estimate=TINY,
        name="line_dot",
    )(rows, weight, *events)


def feed_forward_kernel(
    near_ref, far_ref, grads_near_ref, grads_far_ref, gate_ref, down_ref,
    hid_near_ref, hid_far_ref, dgu_near_ref, dgu_far_ref, dn_near_ref, dn_far_ref, mix_near_ref, mix_far_ref,
):
    rows = jnp.concatenate([near_ref[...], far_ref[...]], axis=0)
    grads = jnp.concatenate([grads_near_ref[...], grads_far_ref[...]], axis=0)
    gate_up = dot(rows, gate_ref[...])
    dhid = dot_nt(grads, down_ref[...])

    def unit(gate, up, grad):
        sig = 1.0 / (1.0 + jnp.exp(-gate))
        act = gate * sig
        return act * up, grad * up * (sig + act * (1.0 - sig)), grad * act

    hid, dgate, dup = unit(
        gate_up[:, :FF_MAIN], gate_up[:, FF_MAIN : 2 * FF_MAIN], dhid[:, :FF_MAIN]
    )
    last = gate_up[:, 2 * FF_MAIN :]
    grad = jnp.concatenate([dhid[:, FF_MAIN:], dhid[:, FF_MAIN:]], axis=1)
    hid_last, dgate_last, dup_last = unit(last, pltpu.roll(last, FF_REST, 1), grad)
    low = lax.broadcasted_iota(jnp.int32, last.shape, 1) < FF_REST
    last = jnp.where(low, dgate_last, pltpu.roll(dup_last, FF_REST, 1))
    hid = hid.astype(BF)
    hid_last = hid_last[:, :FF_REST].astype(BF)
    hid_near_ref[:, :FF_MAIN] = hid[:ROWS]
    hid_near_ref[:, FF_MAIN:] = hid_last[:ROWS]
    hid_far_ref[:, :FF_MAIN] = hid[ROWS:]
    hid_far_ref[:, FF_MAIN:] = hid_last[ROWS:]
    dgu = jnp.concatenate([dgate.astype(BF), dup.astype(BF), last.astype(BF)], axis=1)
    dgu_near_ref[...] = dgu[:ROWS]
    dgu_far_ref[...] = dgu[ROWS:]
    dn = dot_nt(dgu, gate_ref[...]).astype(BF)
    dn_near_ref[...] = dn[:ROWS]
    dn_far_ref[...] = dn[ROWS:]
    mix = dot(jnp.concatenate([hid, hid_last], axis=1), down_ref[...]).astype(BF)
    mix_near_ref[...] = mix[:ROWS]
    mix_far_ref[...] = mix[ROWS:]


def feed_forward(near, far, grads_near, grads_far, gate_full, down_full):
    def side(cols):
        return pl.BlockSpec((ROWS, cols), lambda i: (i, 0))

    outs = (FF_HERE, FF_HERE, 2 * FF_HERE, 2 * FF_HERE, D, D, D, D)
    return pl.pallas_call(
        feed_forward_kernel,
        grid=(4,),
        in_specs=[side(D)] * 4 + [whole(D, 2 * FF_HERE), whole(FF_HERE, D)],
        out_specs=[side(c) for c in outs],
        out_shape=[jax.ShapeDtypeStruct((HALF, c), BF) for c in outs],
        compiler_params=pltpu.CompilerParams(vmem_limit_bytes=VMEM),
        cost_estimate=cost(30e9),
        name="feed_forward",
    )(near, far, grads_near, grads_far, gate_full, down_full)


def weight_grad_kernel(near_ref, far_ref, g_near_ref, g_far_ref, *refs):
    grad = dot_tn(near_ref[...], g_near_ref[...]) + dot_tn(far_ref[...], g_far_ref[...])
    refs[-1][...] = grad.astype(BF)


def weight_grad(near, far, grads_near, grads_far, far_block_index, block, flops, *events):
    deep, cols = near.shape[1], grads_near.shape[1]
    if block == cols:
        grid = deep // 256
        rows = pl.BlockSpec((HALF, 256), lambda i: (0, i))
        grads = [pl.BlockSpec((HALF, cols), lambda i, k=k: (k, 0)) for k in (0, far_block_index)]
        out = pl.BlockSpec((256, cols), lambda i: (i, 0))
    else:
        grid = cols // block
        rows = pl.BlockSpec((HALF, deep), lambda i: (0, 0))
        grads = [pl.BlockSpec((HALF, block), lambda i, k=k: (k, i)) for k in (0, far_block_index)]
        out = pl.BlockSpec((deep, block), lambda i: (0, i))
    return pl.pallas_call(
        weight_grad_kernel,
        grid=(grid,),
        in_specs=[rows, rows, *grads] + [ANY] * len(events),
        out_specs=out,
        out_shape=jax.ShapeDtypeStruct((deep, cols), BF),
        compiler_params=pltpu.CompilerParams(vmem_limit_bytes=VMEM),
        cost_estimate=cost(flops),
        name="weight_grad",
    )(near, far, grads_near, grads_far, *events)


def small_rows(segment_ids, position_ids):
    parts = [position_ids // 32, position_ids % 32, segment_ids // 128, segment_ids % 128]
    flat = jnp.concatenate([p.astype(BF) for p in parts])
    return jnp.pad(flat[None], ((0, 7), (0, PROJ_HERE + 2 * FF_HERE - 512)))


def small_read(rows):
    s = lax.axis_index("shard")
    x, c = (s // 2) % 4, s % 2
    line = rows[:, 0, :512].reshape(4, 2, 4, 128).astype(F32)
    line = lax.dynamic_slice(jnp.concatenate([line, line], axis=0), (x, 0, 0, 0), (4, 2, 4, 128))
    line = jnp.where(c == 0, line, line[:, ::-1]).transpose(1, 0, 2, 3).reshape(8, 4, 128)
    position = (line[:, 0] * 32.0 + line[:, 1]).reshape(TOK)
    segment = (line[:, 2] * 128.0 + line[:, 3]).reshape(TOK)
    return position, segment


def on_device(
    tokens,
    cotangent,
    segment_ids,
    position_ids,
    w_qkv,
    w_out,
    w_gate_up,
    w_down,
    gains,
    m_qkv,
    v_qkv,
    m_out,
    v_out,
    m_gate_up,
    v_gate_up,
    m_down,
    v_down,
    m_gains,
    v_gains,
):
    gain_rows = gains.astype(BF).astype(F32).T
    qkv_low = w_qkv.astype(BF).astype(F32)
    gate_low = w_gate_up.astype(BF).astype(F32)

    with jax.named_scope("qkv_weights_line"):
        low = (qkv_low * gain_rows[:, 0:1]).astype(BF)
        q_cols = low[:, :D].reshape(32, 8, Q_HERE)
        kv_cols = low[:, D:].reshape(32, 2, KV_HEADS, HEAD_DIM).transpose(0, 2, 1, 3)
        kv_cols = jnp.repeat(kv_cols.reshape(32, KV_HEADS, 2 * HEAD_DIM), 2, axis=1)
        qkv_cut = jnp.concatenate([q_cols, kv_cols], axis=2).transpose(1, 0, 2)
    with jax.named_scope("gate_weights_line"):
        low = (gate_low * gain_rows[:, 1:2]).astype(BF)
        low = low.reshape(32, 2, 8, FF_HERE)
        gate_cut = jnp.concatenate(
            [low[:, 0, :, :FF_MAIN], low[:, 1, :, :FF_MAIN], low[:, 0, :, FF_MAIN:], low[:, 1, :, FF_MAIN:]],
            axis=2,
        )
        both = jnp.concatenate([qkv_cut, gate_cut.transpose(1, 0, 2)], axis=2)
        small = small_rows(segment_ids, position_ids)
        small = jnp.broadcast_to(small[None], (8, *small.shape))
        both = line_exchange(jnp.concatenate([both, small], axis=1))
        positions, segments = small_read(both[:, 32:])
        qkv_line = both[:, :32, :PROJ_HERE].reshape(256, PROJ_HERE)
        gate_line = both[:, :32, PROJ_HERE:].reshape(256, 2 * FF_HERE)
    with jax.named_scope("gate_weights_plane"):
        gate_full = plane_gather(gate_line)
    with jax.named_scope("qkv_weights_plane"):
        qkv_full = plane_spread(qkv_line)
    with jax.named_scope("normed_line"):
        normed = unit_norm(tokens.astype(F32)).astype(BF)
        pieces = line_pieces(normed)
        near, far = line_halves(normed, pieces)
    with jax.named_scope("cotangent_line"):
        cot_pieces = line_pieces(after(cotangent, near))
    with jax.named_scope("out_turn"):
        out_turned = turned(w_out.astype(BF))
    with jax.named_scope("down_turn"):
        down_turned = turned(after(w_down.astype(BF), near))
    with jax.named_scope("out_weights_plane"):
        out_full = plane_spread(after(out_turned, qkv_full))
    with jax.named_scope("down_weights_plane"):
        down_full = plane_spread(after(down_turned, out_full))

    freqs = 10000.0 ** (-jnp.arange(HEAD_DIM // 2).astype(F32) * 2.0 / HEAD_DIM)
    angles = positions[:, None] * freqs[None, :]
    cosine = jnp.tile(jnp.cos(angles), (1, 4))
    sine = jnp.sin(angles)
    sine = jnp.concatenate([-sine, sine, -sine, sine], axis=1)
    row = jnp.stack([segments, positions])
    column = row.T
    heads_out, queries, pair, totals = attend(
        near, far, qkv_full, cosine, sine, column, row, *cot_pieces
    )
    with jax.named_scope("cotangent_line"):
        cot_near, cot_far = line_halves(after(cotangent, heads_out), cot_pieces)
    with jax.named_scope("heads_out_line"):
        own, pieces = line_scatter(*line_dot(heads_out, out_full, False, cot_near))
        middle, normed_two = row_kernel(
            middle_kernel, own, pieces, [tokens], [F32, BF], (cot_far, down_full)
        )

    with jax.named_scope("normed_two_line"):
        near_two, far_two = line_halves(normed_two, line_pieces(normed_two))
    hid_near, hid_far, dgu_near, dgu_far, dn_near, dn_far, mix_near, mix_far = feed_forward(
        near_two, far_two, cot_near, cot_far, gate_full, down_full
    )
    with jax.named_scope("grad_gate_plane"):
        grad_gate = weight_grad(near_two, far_two, dgu_near, dgu_far, 0, 2 * FF_HERE, 15e9)
        gate_owned = plane_scatter(grad_gate)
    with jax.named_scope("grad_normed_two_line"):
        own, pieces = line_scatter(dn_near, dn_far, grad_gate)
    with jax.named_scope("grad_down_plane"):
        grad_down = weight_grad(hid_near, hid_far, cot_near, cot_far, 0, 512, 1, own)
        down_parts = plane_exchange(grad_down.reshape(8, 88, D))
    with jax.named_scope("mixed_line"):
        mixed_own, mixed_pieces = line_scatter(mix_near, mix_far)
    with jax.named_scope("grad_normed_two_line"):
        grad_middle, grad_attn = row_kernel(
            middle_back_kernel, own, pieces, [middle, cotangent], [F32, BF], (grad_down, mixed_own)
        )
    with jax.named_scope("grad_attn_line"):
        pieces = line_pieces(grad_attn)
        attn_near, attn_far = line_halves(grad_attn, pieces)
    grad_proj = attend_back(
        attn_near, attn_far, out_full, queries, pair, totals, cosine, sine, column, row,
        mixed_own,
    )
    with jax.named_scope("mixed_line"):
        (mixed,) = row_kernel(mixed_kernel, mixed_own, mixed_pieces, [middle], [F32], (grad_proj,))
    with jax.named_scope("grad_qkv"):
        grad_qkv_local = weight_grad(
            near, far, grad_proj, grad_proj, 1, PROJ_HERE, 5e9, mixed
        )
        qkv_parts = plane_exchange(grad_qkv_local.reshape(8, 256, PROJ_HERE))
    with jax.named_scope("grad_out_plane"):
        grad_out = weight_grad(heads_out[:HALF], heads_out[HALF:], attn_near, attn_far, 0, 512, 1, grad_qkv_local)
    with jax.named_scope("grad_normed_line"):
        own, pieces = line_scatter(*line_dot(grad_proj, qkv_full, True, grad_out, down_parts))
    with jax.named_scope("grad_down_rep"):
        down_owned, down_low = parts_sum(down_parts, 88, pieces[0])
        down_sum = down_owned + come_from(down_low, zz=2).astype(F32)
        grad_down = turned(after(down_sum.astype(BF), pieces[0])).astype(F32)
    with jax.named_scope("grad_gate_rep"):
        gate_low_sum = after(gate_owned, pieces[0])
        gate_from_rep = come_from(gate_low_sum, zz=2)
        gate_sum = gate_low_sum.astype(F32) + gate_from_rep.astype(F32)
    with jax.named_scope("grad_normed_line"):
        (d_tokens,) = row_kernel(
            tokens_back_kernel, own, pieces, [tokens, grad_middle], [F32]
        )
    with jax.named_scope("grad_gate_line"):
        gate_sum = after(gate_sum.astype(BF), pieces[0])
        gate_line_parts = line_exchange(gate_sum.reshape(8, 32, 2 * FF_HERE))
        parts = gate_line_parts.astype(F32)
        main, rest = 2 * FF_MAIN, 2 * FF_MAIN + FF_REST
        grad_gate = jnp.stack(
            [
                jnp.concatenate([parts[:, :, :FF_MAIN], parts[:, :, main:rest]], axis=2),
                jnp.concatenate([parts[:, :, FF_MAIN:main], parts[:, :, rest:]], axis=2),
            ]
        )
        grad_gate = grad_gate.transpose(2, 0, 1, 3).reshape(32, 2 * FF)
    with jax.named_scope("grad_out_rep"):
        out_parts = plane_exchange(after(grad_out.reshape(8, 32, D), gate_line_parts))
        out_owned, out_low = parts_sum(out_parts, 32)
        out_sum = out_owned + come_from(out_low, zz=2).astype(F32)
        grad_out = turned(out_sum.astype(BF)).astype(F32)
    with jax.named_scope("grad_qkv"):
        qkv_sum, qkv_low_sum = parts_sum(qkv_parts, 256, pieces[0])
        qkv_sum = qkv_sum + come_from(qkv_low_sum, zz=2).astype(F32)
        parts = line_exchange(qkv_sum.astype(BF).reshape(8, 32, PROJ_HERE)).astype(F32)
        q_part = parts[:, :, :Q_HERE].transpose(1, 0, 2).reshape(32, D)
        kv_part = parts[:, :, Q_HERE:].reshape(KV_HEADS, 2, 32, 2, HEAD_DIM).sum(axis=1)
        kv_part = kv_part.transpose(1, 2, 0, 3).reshape(32, 2 * KV_HEADS * HEAD_DIM)
        grad_qkv = jnp.concatenate([q_part, kv_part], axis=1)

    grad_gains = jnp.stack(
        [jnp.sum(qkv_low * grad_qkv, axis=1), jnp.sum(gate_low * grad_gate, axis=1)]
    )
    qkv_new = adam_step(w_qkv, grad_qkv * gain_rows[:, 0:1], m_qkv, v_qkv, RATE_QKV)
    out_new = adam_step(w_out, grad_out, m_out, v_out, RATE_OUT)
    gate_new = adam_step(w_gate_up, grad_gate * gain_rows[:, 1:2], m_gate_up, v_gate_up, RATE_GATE_UP)
    down_new = adam_step(w_down, grad_down, m_down, v_down, RATE_DOWN)
    gains_new = adam_step(gains, grad_gains, m_gains, v_gains, RATE_GAINS)
    return (mixed, d_tokens, *qkv_new, *out_new, *gate_new, *down_new, *gains_new)


def solution(mesh):
    tokens = P(BOTH, None)
    ids = P(BOTH)
    rows = P("shard", None)
    columns = P(None, "shard")
    return jax.shard_map(
        on_device,
        mesh=mesh,
        in_specs=(tokens, tokens, ids, ids, rows, rows, rows, rows, columns)
        + (rows,) * 8
        + (columns,) * 2,
        out_specs=(tokens, tokens) + (rows,) * 12 + (columns,) * 3,
        check_vma=False,
    )
```

```python
import functools

import jax
import jax.numpy as jnp
from jax import lax
from jax.experimental import pallas as pl
from jax.experimental.pallas import tpu as pltpu
from jax.sharding import PartitionSpec as P

HEADS = 32
KV_HEADS = 4
HEAD_DIM = 64
D = 2048
FF = 5632
STEP = 10
ROWS = 128
GROUP = 8
TOK = ROWS * GROUP
HALF = TOK // 2
HEADS_HERE = HEADS // GROUP
Q_HERE = HEADS_HERE * HEAD_DIM
PROJ_HERE = Q_HERE + 2 * HEAD_DIM
FF_HERE = FF // GROUP
FF_MAIN = FF_HERE // 128 * 128
FF_REST = FF_HERE - FF_MAIN
Q_BLOCK = 256
VMEM = 60 * 2**20

EPSILON = 1e-05
BETA_ONE = 0.9
BETA_TWO = 0.95
ADAM_EPSILON = 1e-08
DECAY = 0.1
RATE_QKV = 0.02
RATE_OUT = 0.25
RATE_GATE_UP = 0.02
RATE_DOWN = 0.013
RATE_GAINS = 0.3

BF = jnp.bfloat16
F32 = jnp.float32
BOTH = ("rep", "shard")
LINES = [[8 * b + a for a in range(8)] for b in range(8)]
PLANES = [[8 * b + a for b in range(8)] for a in range(8)]


def index_of(r, y, z, x, c):
    return r * 64 + y * 16 + z * 8 + x * 2 + c


def places():
    return [
        (r, y, z, x, c)
        for r in range(2)
        for y in range(4)
        for z in range(2)
        for x in range(4)
        for c in range(2)
    ]


def come_from(v, y=0, x=0, c=0, zz=0):
    pairs = []
    for r, yy, z, xx, cc in places():
        ring = (2 * r + z + zz) % 4
        source = index_of(ring // 2, (yy + y) % 4, ring % 2, (xx + x) % 4, cc ^ c)
        pairs.append((source, index_of(r, yy, z, xx, cc)))
    return lax.ppermute(v, BOTH, pairs)


def turned(v):
    pairs = [(index_of(r, x, c, y, z), index_of(r, y, z, x, c)) for r, y, z, x, c in places()]
    return lax.ppermute(v, BOTH, pairs)


def dot(left, right):
    return jnp.dot(left, right, preferred_element_type=F32)


def dot_nt(left, right):
    return lax.dot_general(left, right, (((1,), (1,)), ((), ())), preferred_element_type=F32)


def dot_tn(left, right):
    return lax.dot_general(left, right, (((0,), (0,)), ((), ())), preferred_element_type=F32)


def after(v, *events):
    for event in events:
        last = event[(-1,) * event.ndim]
        v = jnp.where(last == last, v, jnp.zeros_like(v))
    return v


def settled(v):
    return lax.optimization_barrier(v)


def halves_gather(v):
    pieces = line_pieces(v)
    near, far = line_halves(v, pieces)
    return near, far, pieces[0]


def line_pieces(v):
    return [come_from(v, x=k) for k in (1, 2, 3)]


def line_halves(v, pieces):
    near = settled(jnp.concatenate([v] + pieces, axis=0))
    return near, come_from(near, c=1)


def plane_exchange(v):
    return lax.all_to_all(v, "shard", 0, 0, tiled=True, axis_index_groups=PLANES)


def plane_spread(v):
    parts = plane_exchange(jnp.broadcast_to(v[None], (8, *v.shape)))
    return parts.reshape(8 * v.shape[0], v.shape[1])


def plane_gather(v):
    return lax.all_gather(v, "shard", axis=0, tiled=True, axis_index_groups=PLANES)


def plane_scatter(v):
    return lax.psum_scatter(
        v, "shard", scatter_dimension=0, tiled=True, axis_index_groups=PLANES
    )


def rep_sum(total):
    return total + come_from(total.astype(BF), zz=2).astype(F32)


def line_exchange(v):
    return lax.all_to_all(v, "shard", 0, 0, tiled=True, axis_index_groups=LINES)


def rate_of(values):
    return lax.rsqrt(jnp.mean(values * values, axis=-1, keepdims=True) + EPSILON)


def unit_norm(values):
    return values * rate_of(values)


def unit_norm_back(values, grad):
    rate = rate_of(values)
    unit = values * rate
    return rate * (grad - unit * jnp.mean(grad * unit, axis=-1, keepdims=True))


def adam_step(weight, grad, first, second, rate):
    first_new = BETA_ONE * first + (1.0 - BETA_ONE) * grad
    second_new = BETA_TWO * second + (1.0 - BETA_TWO) * grad * grad
    first_hat = first_new / (1.0 - BETA_ONE**STEP)
    second_hat = second_new / (1.0 - BETA_TWO**STEP)
    weight_new = weight - rate * (
        first_hat / (jnp.sqrt(second_hat) + ADAM_EPSILON) + DECAY * weight
    )
    return (weight_new, first_new, second_new)


TINY = pl.CostEstimate(flops=1, bytes_accessed=1, transcendentals=0)
ANY = pl.BlockSpec(memory_space=pl.ANY)


def cost(flops):
    return pl.CostEstimate(flops=int(flops), bytes_accessed=1, transcendentals=0)


def core_sum_kernel(near_ref, came_ref, *refs):
    own_ref, *piece_refs = refs[-4:]
    total = near_ref[...].astype(F32) + came_ref[...].astype(F32)
    step = pl.program_id(0)

    @pl.when(step == 0)
    def _():
        own_ref[...] = total

    for k in (1, 2, 3):

        @pl.when(step == k)
        def _(k=k):
            piece_refs[k - 1][...] = total.astype(BF)


def line_scatter(near, far, *events):
    here = pl.BlockSpec((ROWS, D), lambda i: (0, 0))
    own, *pieces = pl.pallas_call(
        core_sum_kernel,
        grid=(4,),
        in_specs=[pl.BlockSpec((ROWS, D), lambda i: (i, 0))] * 2 + [ANY] * len(events),
        out_specs=[here] * 4,
        out_shape=[jax.ShapeDtypeStruct((ROWS, D), F32)]
        + [jax.ShapeDtypeStruct((ROWS, D), BF)] * 3,
        cost_estimate=TINY,
        compiler_params=pltpu.CompilerParams(vmem_limit_bytes=VMEM),
        name="core_sum",
    )(near, come_from(far, c=1), *events)
    return own, [come_from(piece, x=-k) for k, piece in zip((1, 2, 3), pieces)]


def pieces_sum(refs):
    total = refs[0][...]
    for ref in refs[1:4]:
        total = total + ref[...].astype(F32)
    return total


def middle_kernel(*refs):
    tokens_ref, middle_ref, normed_ref = refs[4], refs[-2], refs[-1]
    middle = tokens_ref[...].astype(F32) + pieces_sum(refs)
    middle_ref[...] = middle
    normed_ref[...] = unit_norm(middle).astype(BF)


def middle_back_kernel(*refs):
    middle_ref, cotangent_ref, grad_ref, low_ref = refs[4], refs[5], refs[-2], refs[-1]
    grad = cotangent_ref[...].astype(F32) + unit_norm_back(middle_ref[...], pieces_sum(refs))
    grad_ref[...] = grad
    low_ref[...] = grad.astype(BF)


def tokens_back_kernel(*refs):
    tokens_ref, middle_ref, out_ref = refs[4], refs[5], refs[-1]
    out_ref[...] = middle_ref[...] + unit_norm_back(tokens_ref[...].astype(F32), pieces_sum(refs))


def mixed_kernel(*refs):
    refs[-1][...] = refs[4][...] + pieces_sum(refs)


def row_kernel(kernel, own, pieces, others, outs, events=()):
    count = 1 + len(pieces) + len(others)
    spec = pl.BlockSpec((ROWS, D), lambda: (0, 0))
    return pl.pallas_call(
        kernel,
        in_specs=[spec] * count + [ANY] * len(events),
        out_specs=[spec] * len(outs),
        out_shape=[jax.ShapeDtypeStruct((ROWS, D), t) for t in outs],
        cost_estimate=TINY,
        compiler_params=pltpu.CompilerParams(vmem_limit_bytes=VMEM),
        name=kernel.__name__,
    )(own, *pieces, *others, *events)


def parts_sum_kernel(parts_ref, *refs):
    total = parts_ref[0].astype(F32)
    for k in range(1, parts_ref.shape[0]):
        total = total + parts_ref[k].astype(F32)
    refs[-2][...] = total
    refs[-1][...] = total.astype(BF)


def parts_sum(parts, block, *events):
    n, rows, cols = parts.shape
    out = pl.BlockSpec((block, cols), lambda i: (i, 0))
    return pl.pallas_call(
        parts_sum_kernel,
        grid=(rows // block,),
        in_specs=[pl.BlockSpec((n, block, cols), lambda i: (0, i, 0))] + [ANY] * len(events),
        out_specs=[out] * 2,
        out_shape=[jax.ShapeDtypeStruct((rows, cols), t) for t in (F32, BF)],
        cost_estimate=TINY,
        compiler_params=pltpu.CompilerParams(vmem_limit_bytes=VMEM),
        name="parts_sum",
    )(parts, *events)


def lanes(rows):
    return lax.broadcasted_iota(jnp.int32, (rows, 128), 1)


def rotated(v, cosine, sine, lane):
    partner = jnp.where(lane % HEAD_DIM < HEAD_DIM // 2, pltpu.roll(v, 96, 1), pltpu.roll(v, 32, 1))
    return v * cosine + partner * sine


def split_pair(pair, k_ref, v_ref, lane):
    swapped = pltpu.roll(pair, 64, 1)
    low = lane < HEAD_DIM
    zero = jnp.zeros_like(pair)
    k_ref[0] = jnp.where(low, pair, zero).astype(BF)
    k_ref[1] = jnp.where(low, zero, swapped).astype(BF)
    v_ref[0] = jnp.where(low, swapped, zero).astype(BF)
    v_ref[1] = jnp.where(low, zero, pair).astype(BF)


def barred(column_ref, row_ref):
    same = column_ref[:, 0:1] == row_ref[0:1, :]
    before = row_ref[1:2, :] <= column_ref[:, 1:2]
    return jnp.where(same & before, 0.0, -1e30)


def forward_kernel(*refs):
    near_ref, far_ref, w_qkv_ref, cos_ref, sin_ref, cos_all_ref, sin_all_ref, column_ref, row_ref = refs[:9]
    out_ref, q_ref, kv_ref, total_ref, proj_scr, k_scr, v_scr = refs[-7:]
    lane = lanes(Q_BLOCK)
    step = pl.program_id(0)

    @pl.when(step == 0)
    def _():
        for i in range(TOK // Q_BLOCK):
            ref = near_ref if i * Q_BLOCK < HALF else far_ref
            rows = ref[i * Q_BLOCK % HALF : i * Q_BLOCK % HALF + Q_BLOCK]
            proj_scr[i * Q_BLOCK : (i + 1) * Q_BLOCK] = dot(rows, w_qkv_ref[...])
        wide = lanes(TOK)
        pair = proj_scr[:, Q_HERE:]
        turned_pair = rotated(pair, cos_all_ref[...], sin_all_ref[...], wide)
        pair = jnp.where(wide < HEAD_DIM, turned_pair, pair).astype(BF)
        kv_ref[...] = pair
        split_pair(pair.astype(F32), k_scr, v_scr, wide)

    bar = barred(column_ref, row_ref)
    totals = jnp.zeros((Q_BLOCK, 128), F32)
    here = pl.ds(pl.multiple_of(step * Q_BLOCK, Q_BLOCK), Q_BLOCK)
    for chunk in range(HEADS_HERE // 2):
        span = slice(128 * chunk, 128 * (chunk + 1))
        queries = rotated(proj_scr[here, span], cos_ref[...], sin_ref[...], lane).astype(BF)
        queries = (queries.astype(F32) * HEAD_DIM**-0.5).astype(BF)
        q_ref[:, span] = queries
        out = jnp.zeros((Q_BLOCK, 128), F32)
        for side in range(2):
            scores = dot_nt(queries, k_scr[side]) + bar
            peak = jnp.max(scores, axis=1, keepdims=True)
            expo = jnp.exp(scores - peak)
            total = jnp.sum(expo, axis=1, keepdims=True)
            probs = (expo * (1.0 / total)).astype(BF)
            out = out + dot(probs, v_scr[side])
            totals = jnp.where(lane == 2 * chunk + side, peak + jnp.log(total), totals)
        out_ref[:, span] = out.astype(BF)
    total_ref[...] = totals


def backward_kernel(*refs):
    near_ref, far_ref, w_out_ref, q_ref, kv_ref, total_ref, cos_ref, sin_ref, cos_all_ref, sin_all_ref = refs[:10]
    column_ref, row_ref = refs[10:12]
    dproj_ref, do_scr, k_scr, v_scr, dk_scr, dv_scr = refs[-6:]
    lane = lanes(Q_BLOCK)
    step = pl.program_id(0)

    @pl.when(step == 0)
    def _():
        split_pair(kv_ref[...].astype(F32), k_scr, v_scr, lanes(TOK))
        dk_scr[...] = jnp.zeros_like(dk_scr)
        dv_scr[...] = jnp.zeros_like(dv_scr)

    @pl.when(step < HALF // Q_BLOCK)
    def _():
        do_scr[...] = dot_nt(near_ref[...], w_out_ref[...]).astype(BF)

    @pl.when(step >= HALF // Q_BLOCK)
    def _():
        do_scr[...] = dot_nt(far_ref[...], w_out_ref[...]).astype(BF)

    bar = barred(column_ref, row_ref)
    here = pl.ds(pl.multiple_of(step * Q_BLOCK, Q_BLOCK), Q_BLOCK)
    for chunk in range(HEADS_HERE // 2):
        span = slice(128 * chunk, 128 * (chunk + 1))
        queries = q_ref[:, span]
        grads = do_scr[:, span]
        dq = jnp.zeros((Q_BLOCK, 128), F32)
        for side in range(2):
            held = (lane >= HEAD_DIM) == (side == 1)
            head = 2 * chunk + side
            scores = dot_nt(queries, k_scr[side]) + bar
            probs = jnp.exp(scores - total_ref[:, head : head + 1])
            dp = dot_nt(grads, v_scr[side])
            inner = jnp.sum(probs * dp, axis=1, keepdims=True)
            ds = (probs * (dp - inner)).astype(BF)
            dq = dq + dot(ds, k_scr[side])
            dk_scr[...] += dot_tn(ds, jnp.where(held, queries, jnp.zeros_like(queries)))
            dv_scr[...] += dot_tn(
                probs.astype(BF), jnp.where(held, grads, jnp.zeros_like(grads))
            )
        dq = dq * HEAD_DIM**-0.5
        dproj_ref[here, span] = rotated(dq, cos_ref[...], -sin_ref[...], lane).astype(BF)

    @pl.when(step == pl.num_programs(0) - 1)
    def _():
        wide = lanes(TOK)
        dk = dk_scr[...] + pltpu.roll(dk_scr[...], 64, 1)
        dv = dv_scr[...] + pltpu.roll(dv_scr[...], 64, 1)
        dk = rotated(dk, cos_all_ref[...], -sin_all_ref[...], wide)
        dproj_ref[:, Q_HERE:] = jnp.where(wide < HEAD_DIM, dk, dv).astype(BF)


def blocked(cols):
    return pl.BlockSpec((Q_BLOCK, cols), lambda i: (i, 0))


def whole(rows, cols):
    return pl.BlockSpec((rows, cols), lambda i: (0, 0), pipeline_mode=pl.Buffered(1))


def near_block(cols):
    return pl.BlockSpec((Q_BLOCK, cols), lambda i: (jnp.minimum(i, HALF // Q_BLOCK - 1), 0))


def far_block(cols):
    return pl.BlockSpec((Q_BLOCK, cols), lambda i: (jnp.maximum(i - HALF // Q_BLOCK, 0), 0))


def attend(near, far, w_qkv, cosine, sine, column, row, *events):
    return pl.pallas_call(
        forward_kernel,
        grid=(TOK // Q_BLOCK,),
        in_specs=[
            whole(HALF, D),
            whole(HALF, D),
            whole(D, PROJ_HERE),
            blocked(128),
            blocked(128),
            whole(TOK, 128),
            whole(TOK, 128),
            blocked(2),
            whole(2, TOK),
        ]
        + [ANY] * len(events),
        out_specs=[
            blocked(Q_HERE),
            blocked(Q_HERE),
            pl.BlockSpec((TOK, 128), lambda i: (0, 0)),
            blocked(128),
        ],
        out_shape=[
            jax.ShapeDtypeStruct((TOK, Q_HERE), BF),
            jax.ShapeDtypeStruct((TOK, Q_HERE), BF),
            jax.ShapeDtypeStruct((TOK, 128), BF),
            jax.ShapeDtypeStruct((TOK, 128), F32),
        ],
        scratch_shapes=[
            pltpu.VMEM((TOK, PROJ_HERE), F32),
            pltpu.VMEM((2, TOK, 128), BF),
            pltpu.VMEM((2, TOK, 128), BF),
        ],
        compiler_params=pltpu.CompilerParams(vmem_limit_bytes=VMEM),
        cost_estimate=cost(30e9),
        name="attention_forward",
    )(near, far, w_qkv, cosine, sine, cosine, sine, column, row, *events)


def attend_back(near, far, w_out, queries, pair, totals, cosine, sine, column, row, *events):
    return pl.pallas_call(
        backward_kernel,
        grid=(TOK // Q_BLOCK,),
        in_specs=[
            near_block(D),
            far_block(D),
            whole(Q_HERE, D),
            blocked(Q_HERE),
            whole(TOK, 128),
            blocked(128),
            blocked(128),
            blocked(128),
            whole(TOK, 128),
            whole(TOK, 128),
            blocked(2),
            whole(2, TOK),
        ]
        + [ANY] * len(events),
        out_specs=pl.BlockSpec((TOK, PROJ_HERE), lambda i: (0, 0)),
        out_shape=jax.ShapeDtypeStruct((TOK, PROJ_HERE), BF),
        scratch_shapes=[
            pltpu.VMEM((Q_BLOCK, Q_HERE), BF),
            pltpu.VMEM((2, TOK, 128), BF),
            pltpu.VMEM((2, TOK, 128), BF),
            pltpu.VMEM((TOK, 128), F32),
            pltpu.VMEM((TOK, 128), F32),
        ],
        compiler_params=pltpu.CompilerParams(vmem_limit_bytes=VMEM),
        cost_estimate=cost(30e9),
        name="attention_backward",
    )(near, far, w_out, queries, pair, totals, cosine, sine, cosine, sine, column, row, *events)


def line_dot_kernel(*refs, turned_weight):
    rows_ref, w_ref, near_ref, far_ref = refs[0], refs[1], refs[-2], refs[-1]
    product = dot_nt if turned_weight else dot
    part = product(rows_ref[...], w_ref[...]).astype(BF)

    @pl.when(pl.program_id(0) < HALF // Q_BLOCK)
    def _():
        near_ref[...] = part

    @pl.when(pl.program_id(0) >= HALF // Q_BLOCK)
    def _():
        far_ref[...] = part


def line_dot(rows, weight, turned_weight, *events):
    return pl.pallas_call(
        functools.partial(line_dot_kernel, turned_weight=turned_weight),
        grid=(TOK // Q_BLOCK,),
        in_specs=[blocked(rows.shape[1]), whole(*weight.shape)] + [ANY] * len(events),
        out_specs=[near_block(D), far_block(D)],
        out_shape=[jax.ShapeDtypeStruct((HALF, D), BF)] * 2,
        compiler_params=pltpu.CompilerParams(vmem_limit_bytes=VMEM),
        cost_estimate=TINY,
        name="line_dot",
    )(rows, weight, *events)


def feed_forward_kernel(
    near_ref, far_ref, grads_near_ref, grads_far_ref, gate_ref, down_ref,
    hid_near_ref, hid_far_ref, dgu_near_ref, dgu_far_ref, dn_near_ref, dn_far_ref, mix_near_ref, mix_far_ref,
):
    rows = jnp.concatenate([near_ref[...], far_ref[...]], axis=0)
    grads = jnp.concatenate([grads_near_ref[...], grads_far_ref[...]], axis=0)
    gate_up = dot(rows, gate_ref[...])
    dhid = dot_nt(grads, down_ref[...])

    def unit(gate, up, grad):
        sig = 1.0 / (1.0 + jnp.exp(-gate))
        act = gate * sig
        return act * up, grad * up * (sig + act * (1.0 - sig)), grad * act

    hid, dgate, dup = unit(
        gate_up[:, :FF_MAIN], gate_up[:, FF_MAIN : 2 * FF_MAIN], dhid[:, :FF_MAIN]
    )
    last = gate_up[:, 2 * FF_MAIN :]
    grad = jnp.concatenate([dhid[:, FF_MAIN:], dhid[:, FF_MAIN:]], axis=1)
    hid_last, dgate_last, dup_last = unit(last, pltpu.roll(last, FF_REST, 1), grad)
    low = lax.broadcasted_iota(jnp.int32, last.shape, 1) < FF_REST
    last = jnp.where(low, dgate_last, pltpu.roll(dup_last, FF_REST, 1))
    hid = hid.astype(BF)
    hid_last = hid_last[:, :FF_REST].astype(BF)
    hid_near_ref[:, :FF_MAIN] = hid[:ROWS]
    hid_near_ref[:, FF_MAIN:] = hid_last[:ROWS]
    hid_far_ref[:, :FF_MAIN] = hid[ROWS:]
    hid_far_ref[:, FF_MAIN:] = hid_last[ROWS:]
    dgu = jnp.concatenate([dgate.astype(BF), dup.astype(BF), last.astype(BF)], axis=1)
    dgu_near_ref[...] = dgu[:ROWS]
    dgu_far_ref[...] = dgu[ROWS:]
    dn = dot_nt(dgu, gate_ref[...]).astype(BF)
    dn_near_ref[...] = dn[:ROWS]
    dn_far_ref[...] = dn[ROWS:]
    mix = dot(jnp.concatenate([hid, hid_last], axis=1), down_ref[...]).astype(BF)
    mix_near_ref[...] = mix[:ROWS]
    mix_far_ref[...] = mix[ROWS:]


def feed_forward(near, far, grads_near, grads_far, gate_full, down_full):
    def side(cols):
        return pl.BlockSpec((ROWS, cols), lambda i: (i, 0))

    outs = (FF_HERE, FF_HERE, 2 * FF_HERE, 2 * FF_HERE, D, D, D, D)
    return pl.pallas_call(
        feed_forward_kernel,
        grid=(4,),
        in_specs=[side(D)] * 4 + [whole(D, 2 * FF_HERE), whole(FF_HERE, D)],
        out_specs=[side(c) for c in outs],
        out_shape=[jax.ShapeDtypeStruct((HALF, c), BF) for c in outs],
        compiler_params=pltpu.CompilerParams(vmem_limit_bytes=VMEM),
        cost_estimate=cost(30e9),
        name="feed_forward",
    )(near, far, grads_near, grads_far, gate_full, down_full)


def weight_grad_kernel(near_ref, far_ref, g_near_ref, g_far_ref, *refs):
    grad = dot_tn(near_ref[...], g_near_ref[...]) + dot_tn(far_ref[...], g_far_ref[...])
    refs[-1][...] = grad.astype(BF)


def weight_grad(near, far, grads_near, grads_far, far_block_index, block, flops, *events):
    deep, cols = near.shape[1], grads_near.shape[1]
    if block == cols:
        grid = deep // 256
        rows = pl.BlockSpec((HALF, 256), lambda i: (0, i))
        grads = [pl.BlockSpec((HALF, cols), lambda i, k=k: (k, 0)) for k in (0, far_block_index)]
        out = pl.BlockSpec((256, cols), lambda i: (i, 0))
    else:
        grid = cols // block
        rows = pl.BlockSpec((HALF, deep), lambda i: (0, 0))
        grads = [pl.BlockSpec((HALF, block), lambda i, k=k: (k, i)) for k in (0, far_block_index)]
        out = pl.BlockSpec((deep, block), lambda i: (0, i))
    return pl.pallas_call(
        weight_grad_kernel,
        grid=(grid,),
        in_specs=[rows, rows, *grads] + [ANY] * len(events),
        out_specs=out,
        out_shape=jax.ShapeDtypeStruct((deep, cols), BF),
        compiler_params=pltpu.CompilerParams(vmem_limit_bytes=VMEM),
        cost_estimate=cost(flops),
        name="weight_grad",
    )(near, far, grads_near, grads_far, *events)


def small_rows(segment_ids, position_ids):
    parts = [position_ids // 32, position_ids % 32, segment_ids // 128, segment_ids % 128]
    flat = jnp.concatenate([p.astype(BF) for p in parts])
    return jnp.pad(flat[None], ((0, 7), (0, PROJ_HERE + 2 * FF_HERE - 512)))


def small_read(rows):
    s = lax.axis_index("shard")
    x, c = (s // 2) % 4, s % 2
    line = rows[:, 0, :512].reshape(4, 2, 4, 128).astype(F32)
    line = lax.dynamic_slice(jnp.concatenate([line, line], axis=0), (x, 0, 0, 0), (4, 2, 4, 128))
    line = jnp.where(c == 0, line, line[:, ::-1]).transpose(1, 0, 2, 3).reshape(8, 4, 128)
    position = (line[:, 0] * 32.0 + line[:, 1]).reshape(TOK)
    segment = (line[:, 2] * 128.0 + line[:, 3]).reshape(TOK)
    return position, segment


def on_device(
    tokens,
    cotangent,
    segment_ids,
    position_ids,
    w_qkv,
    w_out,
    w_gate_up,
    w_down,
    gains,
    m_qkv,
    v_qkv,
    m_out,
    v_out,
    m_gate_up,
    v_gate_up,
    m_down,
    v_down,
    m_gains,
    v_gains,
):
    gain_rows = gains.astype(BF).astype(F32).T
    qkv_low = w_qkv.astype(BF).astype(F32)
    gate_low = w_gate_up.astype(BF).astype(F32)

    with jax.named_scope("qkv_weights_line"):
        low = (qkv_low * gain_rows[:, 0:1]).astype(BF)
        q_cols = low[:, :D].reshape(32, 8, Q_HERE)
        kv_cols = low[:, D:].reshape(32, 2, KV_HEADS, HEAD_DIM).transpose(0, 2, 1, 3)
        kv_cols = jnp.repeat(kv_cols.reshape(32, KV_HEADS, 2 * HEAD_DIM), 2, axis=1)
        qkv_cut = jnp.concatenate([q_cols, kv_cols], axis=2).transpose(1, 0, 2)
    with jax.named_scope("gate_weights_line"):
        low = (gate_low * gain_rows[:, 1:2]).astype(BF)
        low = low.reshape(32, 2, 8, FF_HERE)
        gate_cut = jnp.concatenate(
            [low[:, 0, :, :FF_MAIN], low[:, 1, :, :FF_MAIN], low[:, 0, :, FF_MAIN:], low[:, 1, :, FF_MAIN:]],
            axis=2,
        )
        both = jnp.concatenate([qkv_cut, gate_cut.transpose(1, 0, 2)], axis=2)
        small = small_rows(segment_ids, position_ids)
        small = jnp.broadcast_to(small[None], (8, *small.shape))
        both = line_exchange(jnp.concatenate([both, small], axis=1))
        positions, segments = small_read(both[:, 32:])
        qkv_line = both[:, :32, :PROJ_HERE].reshape(256, PROJ_HERE)
        gate_line = both[:, :32, PROJ_HERE:].reshape(256, 2 * FF_HERE)
    with jax.named_scope("gate_weights_plane"):
        gate_full = plane_gather(gate_line)
    with jax.named_scope("qkv_weights_plane"):
        qkv_full = plane_spread(qkv_line)
    with jax.named_scope("normed_line"):
        normed = unit_norm(tokens.astype(F32)).astype(BF)
        pieces = line_pieces(normed)
        near, far = line_halves(normed, pieces)
    with jax.named_scope("cotangent_line"):
        cot_pieces = line_pieces(after(cotangent, near))
    with jax.named_scope("out_turn"):
        out_turned = turned(w_out.astype(BF))
    with jax.named_scope("down_turn"):
        down_turned = turned(after(w_down.astype(BF), near))
    with jax.named_scope("out_weights_plane"):
        out_full = plane_spread(after(out_turned, qkv_full))
    with jax.named_scope("down_weights_plane"):
        down_full = plane_spread(after(down_turned, out_full))

    freqs = 10000.0 ** (-jnp.arange(HEAD_DIM // 2).astype(F32) * 2.0 / HEAD_DIM)
    angles = positions[:, None] * freqs[None, :]
    cosine = jnp.tile(jnp.cos(angles), (1, 4))
    sine = jnp.sin(angles)
    sine = jnp.concatenate([-sine, sine, -sine, sine], axis=1)
    row = jnp.stack([segments, positions])
    column = row.T
    heads_out, queries, pair, totals = attend(
        near, far, qkv_full, cosine, sine, column, row, *cot_pieces
    )
    with jax.named_scope("cotangent_line"):
        cot_near, cot_far = line_halves(after(cotangent, heads_out), cot_pieces)
    with jax.named_scope("heads_out_line"):
        own, pieces = line_scatter(*line_dot(heads_out, out_full, False, cot_near))
        middle, normed_two = row_kernel(
            middle_kernel, own, pieces, [tokens], [F32, BF], (cot_far, down_full)
        )

    with jax.named_scope("normed_two_line"):
        near_two, far_two = line_halves(normed_two, line_pieces(normed_two))
    hid_near, hid_far, dgu_near, dgu_far, dn_near, dn_far, mix_near, mix_far = feed_forward(
        near_two, far_two, cot_near, cot_far, gate_full, down_full
    )
    with jax.named_scope("grad_gate_plane"):
        grad_gate = weight_grad(near_two, far_two, dgu_near, dgu_far, 0, 2 * FF_HERE, 15e9)
        gate_owned = plane_scatter(grad_gate)
    with jax.named_scope("grad_normed_two_line"):
        own, pieces = line_scatter(dn_near, dn_far, grad_gate)
    with jax.named_scope("grad_down_plane"):
        grad_down = weight_grad(hid_near, hid_far, cot_near, cot_far, 0, 512, 1, own)
    with jax.named_scope("mixed_line"):
        mixed_own, mixed_pieces = line_scatter(mix_near, mix_far)
    with jax.named_scope("grad_normed_two_line"):
        grad_middle, grad_attn = row_kernel(
            middle_back_kernel, own, pieces, [middle, cotangent], [F32, BF], (grad_down, mixed_own)
        )
    with jax.named_scope("grad_attn_line"):
        pieces = line_pieces(grad_attn)
        attn_near, attn_far = line_halves(grad_attn, pieces)
    with jax.named_scope("grad_out_down_plane"):
        grad_out = weight_grad(heads_out[:HALF], heads_out[HALF:], attn_near, attn_far, 0, 512, 1)
        grad_out_down = jnp.concatenate([grad_out.reshape(8, 32, D), grad_down.reshape(8, 88, D)], axis=1)
        od_parts = plane_exchange(grad_out_down)

    grad_proj = attend_back(
        attn_near, attn_far, out_full, queries, pair, totals, cosine, sine, column, row,
        mixed_own,
    )
    with jax.named_scope("mixed_line"):
        (mixed,) = row_kernel(mixed_kernel, mixed_own, mixed_pieces, [middle], [F32], (grad_proj,))
    with jax.named_scope("grad_qkv"):
        grad_qkv_local = weight_grad(
            near, far, grad_proj, grad_proj, 1, PROJ_HERE, 5e9, mixed
        )
        qkv_parts = plane_exchange(grad_qkv_local.reshape(8, 256, PROJ_HERE))
    with jax.named_scope("grad_normed_line"):
        own, pieces = line_scatter(*line_dot(grad_proj, qkv_full, True, grad_qkv_local, od_parts))
    with jax.named_scope("grad_out_down_rep"):
        od_owned, od_low = parts_sum(od_parts, 120, pieces[0])
        od_sum = od_owned + come_from(od_low, zz=2).astype(F32)
        grad_out_down = turned(od_sum.astype(BF)).astype(F32)
        grad_out, grad_down = grad_out_down[:32], grad_out_down[32:]
    with jax.named_scope("grad_gate_rep"):
        gate_low_sum = after(gate_owned, pieces[0])
        gate_from_rep = come_from(gate_low_sum, zz=2)
        gate_sum = gate_low_sum.astype(F32) + gate_from_rep.astype(F32)
    with jax.named_scope("grad_normed_line"):
        (d_tokens,) = row_kernel(
            tokens_back_kernel, own, pieces, [tokens, grad_middle], [F32]
        )
    with jax.named_scope("grad_gate_line"):
        gate_sum = after(gate_sum.astype(BF), pieces[0])
        gate_line_parts = line_exchange(gate_sum.reshape(8, 32, 2 * FF_HERE))
        parts = gate_line_parts.astype(F32)
        main, rest = 2 * FF_MAIN, 2 * FF_MAIN + FF_REST
        grad_gate = jnp.stack(
            [
                jnp.concatenate([parts[:, :, :FF_MAIN], parts[:, :, main:rest]], axis=2),
                jnp.concatenate([parts[:, :, FF_MAIN:main], parts[:, :, rest:]], axis=2),
            ]
        )
        grad_gate = grad_gate.transpose(2, 0, 1, 3).reshape(32, 2 * FF)
    with jax.named_scope("grad_qkv"):
        qkv_sum, qkv_low_sum = parts_sum(qkv_parts, 256, pieces[0])
        qkv_sum = qkv_sum + come_from(qkv_low_sum, zz=2).astype(F32)
        parts = line_exchange(qkv_sum.astype(BF).reshape(8, 32, PROJ_HERE)).astype(F32)
        q_part = parts[:, :, :Q_HERE].transpose(1, 0, 2).reshape(32, D)
        kv_part = parts[:, :, Q_HERE:].reshape(KV_HEADS, 2, 32, 2, HEAD_DIM).sum(axis=1)
        kv_part = kv_part.transpose(1, 2, 0, 3).reshape(32, 2 * KV_HEADS * HEAD_DIM)
        grad_qkv = jnp.concatenate([q_part, kv_part], axis=1)

    grad_gains = jnp.stack(
        [jnp.sum(qkv_low * grad_qkv, axis=1), jnp.sum(gate_low * grad_gate, axis=1)]
    )
    qkv_new = adam_step(w_qkv, grad_qkv * gain_rows[:, 0:1], m_qkv, v_qkv, RATE_QKV)
    out_new = adam_step(w_out, grad_out, m_out, v_out, RATE_OUT)
    gate_new = adam_step(w_gate_up, grad_gate * gain_rows[:, 1:2], m_gate_up, v_gate_up, RATE_GATE_UP)
    down_new = adam_step(w_down, grad_down, m_down, v_down, RATE_DOWN)
    gains_new = adam_step(gains, grad_gains, m_gains, v_gains, RATE_GAINS)
    return (mixed, d_tokens, *qkv_new, *out_new, *gate_new, *down_new, *gains_new)


def solution(mesh):
    tokens = P(BOTH, None)
    ids = P(BOTH)
    rows = P("shard", None)
    columns = P(None, "shard")
    return jax.shard_map(
        on_device,
        mesh=mesh,
        in_specs=(tokens, tokens, ids, ids, rows, rows, rows, rows, columns)
        + (rows,) * 8
        + (columns,) * 2,
        out_specs=(tokens, tokens) + (rows,) * 12 + (columns,) * 3,
        check_vma=False,
    )
```
